512 devices in a mesh: src: 16 (over y_hi, x, core), dst: 32 (over z, y_lo).
Axes of the slice: x: 4, y: 4 (y_hi: 2, y_lo: 2; y = y_hi * 2 + y_lo), z: 16, core: 2. Of those that a mesh axis runs over, the one named last changes fastest.
Arguments:
- features: bfloat16 [98304, 256], P(('src', 'dst')), may hold values from -6 to 6
- weight: bfloat16 [256, 256], replicated, may hold values from -0.375 to 0.375
- values: bfloat16 [16, 32, 144, 128, 128], P('src', 'dst'), may hold values from -0.109375 to 0.109375
- coords: int32 [16, 32, 144, 2], P('src', 'dst'), may hold values from 0 to 47, as said below
- counts: int32 [16, 32], P('src', 'dst'), may hold values from 1 to 144, as said below
- cotangent: bfloat16 [32, 3072, 256], P('dst', 'src'), may hold values from -6 to 6
Outputs:
- activations: bfloat16 [32, 3072, 256], P('dst', 'src')
- input_grad: bfloat16 [98304, 256], P(('src', 'dst'))
- weight_grad: float32 [256, 256], replicated
The draws below stay inside these ranges and needn't reach their ends.
Inputs may be any that keep to these rules, and one draw needn't show every extreme that they name: coords[s, d, k, 0] is below 48 and coords[s, d, k, 1] below 24; the 144 slots of one tile name distinct blocks; slots from counts[s, d] on are not part of the graph. `counts`: some tile holds exactly 144 blocks.
All inputs are finite; a program needn't handle non-finite values.
Results may differ from the reference program's by a relative error of at most 0.03.
Values may be sent and summed in bfloat16 or wider, within the bound.
No kernel may reach another device: no remote copies, remote signals or barrier semaphores. Data moves between devices by JAX's collectives and lax.ppermute only.
A program may use at most 128 MiB of HBM per device.

```python
import jax
import jax.numpy as jnp
from jax import lax

F = 256
BLK = 128
DB = 24
SB = 48
KMAX = 144
ND = 3072
NS = 6144
NODES = 98304
N_SRC = 16
N_DST = 32


def draw_coords(key, part):
    key = jax.random.fold_in(key, 11)
    positions = SB * DB
    scores = jax.random.randint(key, (N_SRC, N_DST, positions), 0, 1 << 20) * positions + jnp.arange(positions, dtype=jnp.int32)
    picked_cells = jnp.argsort(scores, axis=-1, stable=True)[..., :KMAX].astype(jnp.int32)
    return jnp.stack([picked_cells // DB, picked_cells % DB], axis=-1).astype(jnp.int32)


def draw_counts(key, part):
    key = jax.random.fold_in(key, 23)
    first_key, second_key, third_key = jax.random.split(key, 3)
    light = jax.random.randint(first_key, (N_SRC, N_DST), 1, KMAX // 2 + 1)
    heavy = jax.random.randint(second_key, (N_SRC, N_DST), 0, 8) == 0
    chosen = jax.random.randint(third_key, (), 0, N_SRC * N_DST)
    tile_ids = jnp.arange(N_SRC * N_DST, dtype=jnp.int32).reshape(N_SRC, N_DST)
    return jnp.where(heavy | (tile_ids == chosen), KMAX, light).astype(jnp.int32)


def level_of(rng, shape, cuts, least, top_value):
    def one(position, parts):
        heights = jax.random.uniform(jax.random.fold_in(jax.random.fold_in(rng, 6), position), (parts,), jnp.float32, least / len(cuts), top_value / len(cuts))
        return jnp.repeat(jnp.exp(heights), shape[position] // parts).reshape((-1,) + (1,) * (len(shape) - position - 1))

    gain = one(*cuts[0])
    for cut in cuts[1:]:
        gain = gain * one(*cut)
    return gain


def noise(rng, shape, scale, most, shards=(), kind=jnp.bfloat16):
    array = jax.random.normal(rng, shape, jnp.float32) * scale
    if len(shards) > 0:
        array = level_of(rng, shape, shards, -0.22, 0.18) * array
    return jnp.clip(array, min=-most, max=most).astype(kind)


def setup_inputs(seed: int = 0) -> dict:
    streams_of = jax.random.split(jax.random.key(seed), 7)
    return {
        "features": noise(streams_of[0], (NODES, F), 1.0, 6.0, ((0, 512),)),
        "weight": noise(streams_of[1], (F, F), F ** -0.5, 0.375),
        "values": noise(streams_of[2], (N_SRC, N_DST, KMAX, BLK, BLK), (KMAX * BLK * N_SRC // (4 * DB)) ** -0.5, 0.109375, ((0, 16), (1, 32))),
        "coords": draw_coords(jax.random.fold_in(streams_of[6], 71), 0),
        "counts": draw_counts(jax.random.fold_in(streams_of[6], 71), 0),
        "cotangent": noise(streams_of[5], (N_DST, ND, F), 1.0, 6.0, ((0, 32), (1, 16))),
    }


def tile_forward(tile_values, tile_coords, tile_count, source_rows):
    picked = jnp.take(source_rows, tile_coords[:, 0], axis=0).astype(jnp.float32)
    products = jnp.einsum('kij,kif->kjf', tile_values.astype(jnp.float32), picked)
    is_live = jnp.arange(KMAX, dtype=jnp.int32) < tile_count
    table = ((tile_coords[:, 1][None, :] == jnp.arange(DB, dtype=jnp.int32)[:, None]) & is_live[None, :]).astype(jnp.float32)
    return jnp.einsum('bk,kjf->bjf', table, products, precision=lax.Precision.HIGHEST)


def tile_backward(tile_values, tile_coords, tile_count, dest_rows):
    picked = jnp.take(dest_rows, tile_coords[:, 1], axis=0).astype(jnp.float32)
    products = jnp.einsum('kij,kjf->kif', tile_values.astype(jnp.float32), picked)
    is_live = jnp.arange(KMAX, dtype=jnp.int32) < tile_count
    table = ((tile_coords[:, 0][None, :] == jnp.arange(SB, dtype=jnp.int32)[:, None]) & is_live[None, :]).astype(jnp.float32)
    return jnp.einsum('ak,kif->aif', table, products, precision=lax.Precision.HIGHEST)


def reference(features, weight, values, coords, counts, cotangent):
    source_blocks = features.reshape(N_SRC, SB, BLK, F)

    def one_column(column):
        def accumulate(running, row_index):
            piece = tile_forward(values[row_index, column], coords[row_index, column], counts[row_index, column], source_blocks[row_index])
            piece = lax.optimization_barrier(piece.astype(jnp.bfloat16)).astype(jnp.float32)
            return running + piece, None
        summed, _ = lax.scan(accumulate, jnp.zeros((DB, BLK, F), jnp.float32), jnp.arange(N_SRC, dtype=jnp.int32))
        return summed.astype(jnp.bfloat16).reshape(ND, F)

    aggregated = lax.map(one_column, jnp.arange(N_DST, dtype=jnp.int32))
    flat_agg = aggregated.reshape(NODES, F)
    preact = jnp.dot(flat_agg, weight, preferred_element_type=jnp.float32)
    sigma = jax.nn.sigmoid(preact)
    activations = (preact * sigma).astype(jnp.bfloat16).reshape(N_DST, ND, F)
    slope = sigma * (1.0 + preact * (1.0 - sigma))
    delta = (cotangent.reshape(NODES, F).astype(jnp.float32) * slope).astype(jnp.bfloat16)
    weight_grad = jnp.dot(flat_agg.T, delta, preferred_element_type=jnp.float32)
    grad_agg = jnp.dot(delta, weight.T, preferred_element_type=jnp.float32).astype(jnp.bfloat16)
    dest_blocks = grad_agg.reshape(N_DST, DB, BLK, F)

    def one_row(row_index):
        def accumulate(running, column):
            piece = tile_backward(values[row_index, column], coords[row_index, column], counts[row_index, column], dest_blocks[column])
            piece = lax.optimization_barrier(piece.astype(jnp.bfloat16)).astype(jnp.float32)
            return running + piece, None
        summed, _ = lax.scan(accumulate, jnp.zeros((SB, BLK, F), jnp.float32), jnp.arange(N_DST, dtype=jnp.int32))
        return summed.astype(jnp.bfloat16).reshape(NS, F)

    input_grad = lax.map(one_row, jnp.arange(N_SRC, dtype=jnp.int32)).reshape(NODES, F)
    return activations, input_grad, weight_grad
```

```python
import functools

import jax
import jax.numpy as jnp
from jax import lax
from jax.experimental import pallas as pl
from jax.experimental.pallas import tpu as pltpu
from jax.sharding import PartitionSpec as P

BF16 = jnp.bfloat16
F32 = jnp.float32
NZ, NY = 16, 2
N_SRC = 16
SIDE = 128
WIDTH = 256
ROWS = 192
PAIR = NY * ROWS
GROUP = 16
VMEM_LIMIT = 40 * 1024 * 1024

STRIDE_GROUPS = [[2 * z + y for z in range(q, NZ, 4)] for q in range(4) for y in range(NY)]
Y_GROUPS = [[2 * z, 2 * z + 1] for z in range(NZ)]


def from_z(step):
    return [(((z + step) % NZ) * NY + y, z * NY + y) for z in range(NZ) for y in range(NY)]


Y_SWAP = [(d, d ^ 1) for d in range(NZ * NY)]


def live_slots(slot_count, values_ref, held, sems, one_slot):
    slots = values_ref.shape[0]
    groups = slots // GROUP

    def copy(g):
        span = pl.ds(g * GROUP, GROUP)
        return pltpu.make_async_copy(values_ref.at[span], held.at[span], sems.at[g])

    def start():
        for g in range(groups):

            @pl.when(g * GROUP < slot_count)
            def _():
                copy(g).start()

    def run():
        for g in range(groups):

            @pl.when(g * GROUP < slot_count)
            def _():
                copy(g).wait()
                live = jnp.minimum(slot_count - g * GROUP, GROUP)

                def four(i, carry):
                    one_slot([g * GROUP + 4 * i + u for u in range(4)])
                    return carry

                def single(i, carry):
                    one_slot([g * GROUP + i])
                    return carry

                lax.fori_loop(0, live // 4, four, 0)
                lax.fori_loop((live // 4) * 4, live, single, 0)

    return start, run


def block_of(ref, index):
    return ref[pl.ds(pl.multiple_of(index * SIDE, SIDE), SIDE), :]


def add_block(ref, index, term):
    span = pl.ds(pl.multiple_of(index * SIDE, SIDE), SIDE)
    ref[span, :] = ref[span, :] + term


def forward_kernel(
    meta, coords, values_ref, g0, g1, g2a, g2b, g3, out_ref, held, rows, total, value_sems, row_sems
):
    slot_count, z = meta[0], meta[1]
    slots = values_ref.shape[0]

    def one_slot(ks):
        terms = [
            lax.dot_general(
                held[k], block_of(rows, coords[k]), (((0,), (0,)), ((), ())), preferred_element_type=F32
            )
            for k in ks
        ]
        for k, term in zip(ks, terms):
            add_block(total, coords[slots + k], term)

    start, run = live_slots(slot_count, values_ref, held, value_sems, one_slot)
    copies = []
    for offset, ref, first in ((0, g0, 0), (1, g1, 0), (3, g3, 0), (2, g2a, 0), (2, g2b, 2)):
        residue = lax.rem(z + offset, 4)
        for i in range(ref.shape[0]):
            place = (residue + 4 * (first + i)) * PAIR
            copies.append(
                pltpu.make_async_copy(
                    ref.at[i],
                    rows.at[pl.ds(pl.multiple_of(place, PAIR), PAIR)],
                    row_sems.at[len(copies)],
                )
            )
    for copy in copies:
        copy.start()
    start()
    total[...] = jnp.zeros_like(total)
    for copy in copies:
        copy.wait()
    run()
    out_ref[...] = total[...].astype(BF16)


def forward_sums(meta, coords, values, parts, dest_rows):
    slots = values.shape[0]
    source_rows = NZ * PAIR
    smem = pl.BlockSpec(memory_space=pltpu.SMEM)
    anywhere = pl.BlockSpec(memory_space=pl.ANY)
    return pl.pallas_call(
        forward_kernel,
        out_shape=jax.ShapeDtypeStruct((dest_rows, WIDTH), BF16),
        in_specs=[smem, smem] + [anywhere] * 6,
        out_specs=pl.BlockSpec(memory_space=pltpu.VMEM),
        scratch_shapes=[
            pltpu.VMEM(values.shape, BF16),
            pltpu.VMEM((source_rows, WIDTH), BF16),
            pltpu.VMEM((dest_rows, WIDTH), F32),
            pltpu.SemaphoreType.DMA((slots // GROUP,)),
            pltpu.SemaphoreType.DMA((NZ,)),
        ],
        compiler_params=pltpu.CompilerParams(vmem_limit_bytes=VMEM_LIMIT),
        name="forward_sums",
    )(meta, coords, values, *parts)


def middle_kernel(terms, weight, cotangent, act_ref, message):
    agg = jnp.sum(terms[...].astype(F32), axis=0).astype(BF16)
    w = weight[...]
    preact = jnp.dot(agg, w, preferred_element_type=F32)
    sigma = jax.nn.sigmoid(preact)
    act_ref[...] = (preact * sigma).astype(BF16)
    slope = sigma * (1.0 + preact * (1.0 - sigma))
    delta = (cotangent[...].astype(F32) * slope).astype(BF16)
    grad_agg = lax.dot_general(
        delta, w, (((1,), (1,)), ((), ())), preferred_element_type=F32
    ).astype(BF16)
    local = lax.dot_general(agg, delta, (((0,), (0,)), ((), ())), preferred_element_type=F32)
    share = WIDTH // N_SRC
    for s in range(N_SRC):
        message[s, :ROWS, :] = grad_agg
        message[s, ROWS:, :] = local[s * share : (s + 1) * share, :].astype(BF16)


def middle(terms, weight, cotangent):
    share = WIDTH // N_SRC
    vmem = pl.BlockSpec(memory_space=pltpu.VMEM)
    return pl.pallas_call(
        middle_kernel,
        out_shape=(
            jax.ShapeDtypeStruct((ROWS, WIDTH), BF16),
            jax.ShapeDtypeStruct((N_SRC, ROWS + share, WIDTH), BF16),
        ),
        in_specs=[vmem] * 3,
        out_specs=(vmem, vmem),
        compiler_params=pltpu.CompilerParams(vmem_limit_bytes=VMEM_LIMIT),
        name="middle",
    )(terms, weight, cotangent)


def backward_kernel(
    meta, coords, values_ref, message, p0, p1a, p1b, p3a, p3b, p2a, p2b, wsum,
    held, rows, total, tail, value_sems, row_sems, tail_sem,
):
    slot_count, z, y = meta[0], meta[1], meta[2]
    slots = values_ref.shape[0]

    def one_slot(ks):
        terms = [
            jnp.dot(held[k], block_of(rows, coords[slots + k]), preferred_element_type=F32)
            for k in ks
        ]
        for k, term in zip(ks, terms):
            add_block(total, coords[k], term)

    start, run = live_slots(slot_count, values_ref, held, value_sems, one_slot)
    copies = [
        pltpu.make_async_copy(
            message.at[s, pl.ds(0, ROWS)], rows.at[pl.ds(s * ROWS, ROWS)], row_sems.at[s]
        )
        for s in range(N_SRC)
    ]
    share = message.shape[1] - ROWS
    tail_copy = pltpu.make_async_copy(message.at[:, pl.ds(ROWS, share)], tail, tail_sem)
    for copy in copies:
        copy.start()
    tail_copy.start()
    start()
    total[...] = jnp.zeros_like(total)
    for copy in copies:
        copy.wait()
    tail_copy.wait()
    run()
    summed = jnp.sum(tail[...].astype(F32), axis=0)
    wsum[...] = summed
    p2b[4 * ROWS :, :] = summed.astype(BF16)

    def put(ref, first_row, offset, member, other):
        place = (lax.rem(z + offset, 4) + 4 * member) * PAIR + (y if other == 0 else 1 - y) * ROWS
        chunk = total[pl.ds(pl.multiple_of(place, ROWS), ROWS), :]
        ref[first_row : first_row + ROWS, :] = chunk.astype(BF16)

    for other in range(2):
        for member in range(4):
            put(p0, (other * 4 + member) * ROWS, 0, member, other)
        for i in range(2):
            place = (other * 2 + i) * ROWS
            put(p1a, place, 1, i, other)
            put(p1b, place, 1, 2 + i, other)
            put(p3a, place, 3, i, other)
            put(p3b, place, 3, 2 + i, other)
            put(p2a, place, 2, i, other)
            put(p2b, place, 2, 2 + i, other)


def backward_sums(meta, coords, values, message):
    slots = values.shape[0]
    share = message.shape[1] - ROWS
    dest_rows = N_SRC * ROWS
    source_rows = NZ * PAIR
    smem = pl.BlockSpec(memory_space=pltpu.SMEM)
    anywhere = pl.BlockSpec(memory_space=pl.ANY)
    vmem = pl.BlockSpec(memory_space=pltpu.VMEM)
    half = jax.ShapeDtypeStruct((4 * ROWS, WIDTH), BF16)
    return pl.pallas_call(
        backward_kernel,
        out_shape=(
            jax.ShapeDtypeStruct((8 * ROWS, WIDTH), BF16),
            half, half, half, half, half,
            jax.ShapeDtypeStruct((4 * ROWS + share, WIDTH), BF16),
            jax.ShapeDtypeStruct((share, WIDTH), F32),
        ),
        in_specs=[smem, smem, anywhere, anywhere],
        out_specs=(vmem,) * 8,
        scratch_shapes=[
            pltpu.VMEM(values.shape, BF16),
            pltpu.VMEM((dest_rows, WIDTH), BF16),
            pltpu.VMEM((source_rows, WIDTH), F32),
            pltpu.VMEM((N_SRC, share, WIDTH), BF16),
            pltpu.SemaphoreType.DMA((slots // GROUP,)),
            pltpu.SemaphoreType.DMA((N_SRC,)),
            pltpu.SemaphoreType.DMA,
        ],
        compiler_params=pltpu.CompilerParams(vmem_limit_bytes=VMEM_LIMIT),
        name="backward_sums",
    )(meta, coords, values, message)


def shift(array, step):
    return lax.ppermute(array, "dst", from_z(step))


def gather_sources(features):
    own = lax.all_gather(features, "dst", axis=0, axis_index_groups=STRIDE_GROUPS)
    own = lax.all_gather(own, "dst", axis=1, tiled=True, axis_index_groups=Y_GROUPS)
    right = shift(own, 1)
    left = shift(own, -1)
    far_low = shift(right[:2], 1)
    far_high = shift(left[2:], -1)
    return own, right, far_low, far_high, left


def scatter_sources(p0, p1a, p1b, p3a, p3b, p2a, p2b, wsum):
    half = 4 * ROWS
    low = shift(p2a, -1)
    high = shift(p2b, 1)
    w1 = wsum + high[half:].astype(F32)
    w1_sent = w1.astype(BF16)
    up = jnp.concatenate([(p1a.astype(F32) + low.astype(F32)).astype(BF16), p1b, w1_sent], 0)
    down = jnp.concatenate([p3a, (p3b.astype(F32) + high[:half].astype(F32)).astype(BF16), w1_sent], 0)
    from_below = shift(up, -1)
    from_above = shift(down, 1)
    w2 = from_below[2 * half :].astype(F32) + from_above[2 * half :].astype(F32)

    def both(span):
        return from_below[span].astype(F32) + from_above[span].astype(F32)

    quarter = half // 2
    near = jnp.concatenate([both(slice(0, quarter)), both(slice(half, half + quarter))], 0)
    away = jnp.concatenate([both(slice(quarter, half)), both(slice(half + quarter, 2 * half))], 0)
    kept = p0[:half].astype(F32) + near
    sent = (p0[half:].astype(F32) + away).astype(BF16)
    sent = jnp.concatenate([sent, w2.astype(BF16)], 0)
    got = lax.ppermute(sent, "dst", Y_SWAP)
    w3 = (w2 + got[half:].astype(F32)).astype(BF16)
    mine = (kept + got[:half].astype(F32)).astype(BF16).reshape(4, ROWS, WIDTH)
    message = jnp.concatenate([mine, jnp.broadcast_to(w3, (4,) + w3.shape)], 1)
    last = lax.all_to_all(message, "dst", 0, 0, tiled=True, axis_index_groups=STRIDE_GROUPS)
    last = jnp.sum(last.astype(F32), axis=0)
    return last[:ROWS].astype(BF16), last[ROWS:]


def shards(features, weight, values, coords, counts, cotangent):
    tile_values = values[0, 0]
    pairs = coords[0, 0].T.reshape(-1)
    place = lax.axis_index("dst")
    meta = jnp.stack([counts[0, 0], place // NY, lax.rem(place, NY)]).astype(jnp.int32)
    dest_rows = cotangent.shape[1] * N_SRC

    parts = gather_sources(features)
    terms = forward_sums(meta, pairs, tile_values, parts, dest_rows)
    terms = lax.all_to_all(terms.reshape(N_SRC, ROWS, WIDTH), "src", 0, 0, tiled=True)
    activations, message = middle(terms, weight, cotangent[0])
    message = lax.all_to_all(message, "src", 0, 0, tiled=True)
    sums = backward_sums(meta, pairs, tile_values, message)
    input_grad, weight_part = scatter_sources(*sums)
    share = weight_part.shape[0]
    weight_part = jnp.broadcast_to(weight_part, (N_SRC, share, WIDTH))
    weight_grad = lax.all_to_all(weight_part, "src", 0, 0, tiled=True).reshape(WIDTH, WIDTH)
    return (activations[None], input_grad, weight_grad)


def solution(mesh):
    in_specs = (
        P(("src", "dst"), None),
        P(),
        P("src", "dst", None, None, None),
        P("src", "dst", None, None),
        P("src", "dst"),
        P("dst", "src", None),
    )
    out_specs = (P("dst", "src", None), P(("src", "dst"), None), P())
    return jax.shard_map(shards, mesh=mesh, in_specs=in_specs, out_specs=out_specs, check_vma=False)
```

```python
import functools

import jax
import jax.numpy as jnp
from jax import lax
from jax.experimental import pallas as pl
from jax.experimental.pallas import tpu as pltpu
from jax.sharding import PartitionSpec as P

BF16 = jnp.bfloat16
F32 = jnp.float32
NZ, NY = 16, 2
N_SRC = 16
SIDE = 128
WIDTH = 256
ROWS = 192
PAIR = NY * ROWS
GROUP = 16
VMEM_LIMIT = 40 * 1024 * 1024

STRIDE_GROUPS = [[2 * z + y for z in range(q, NZ, 4)] for q in range(4) for y in range(NY)]
Y_GROUPS = [[2 * z, 2 * z + 1] for z in range(NZ)]
CHIPS = N_SRC // 2
CORE_GROUPS = [[2 * chip + core for chip in range(CHIPS)] for core in range(2)]
CORE_SWAP = [(s, s ^ 1) for s in range(N_SRC)]


def from_z(step):
    return [(((z + step) % NZ) * NY + y, z * NY + y) for z in range(NZ) for y in range(NY)]


def live_slots(slot_count, values_ref, held, sems, one_slot):
    slots = values_ref.shape[0]
    groups = slots // GROUP

    def copy(g):
        span = pl.ds(g * GROUP, GROUP)
        return pltpu.make_async_copy(values_ref.at[span], held.at[span], sems.at[g])

    def start():
        for g in range(groups):

            @pl.when(g * GROUP < slot_count)
            def _():
                copy(g).start()

    def run():
        for g in range(groups):

            @pl.when(g * GROUP < slot_count)
            def _():
                copy(g).wait()
                live = jnp.minimum(slot_count - g * GROUP, GROUP)

                def four(i, carry):
                    one_slot([g * GROUP + 4 * i + u for u in range(4)])
                    return carry

                def single(i, carry):
                    one_slot([g * GROUP + i])
                    return carry

                lax.fori_loop(0, live // 4, four, 0)
                lax.fori_loop((live // 4) * 4, live, single, 0)

    return start, run


def block_of(ref, index):
    return ref[pl.ds(pl.multiple_of(index * SIDE, SIDE), SIDE), :]


def add_block(ref, index, term):
    span = pl.ds(pl.multiple_of(index * SIDE, SIDE), SIDE)
    ref[span, :] = ref[span, :] + term


def forward_kernel(
    meta, coords, values_ref, g0, g1, g2a, g2b, g3, own, other, held, rows, total, value_sems, row_sems
):
    slot_count, z, core = meta[0], meta[1], meta[3]
    slots = values_ref.shape[0]

    def one_slot(ks):
        terms = [
            lax.dot_general(
                held[k], block_of(rows, coords[k]), (((0,), (0,)), ((), ())), preferred_element_type=F32
            )
            for k in ks
        ]
        for k, term in zip(ks, terms):
            add_block(total, coords[slots + k], term)

    start, run = live_slots(slot_count, values_ref, held, value_sems, one_slot)
    copies = []
    for offset, ref, first in ((0, g0, 0), (1, g1, 0), (3, g3, 0), (2, g2a, 0), (2, g2b, 2)):
        residue = lax.rem(z + offset, 4)
        for i in range(ref.shape[0]):
            place = (residue + 4 * (first + i)) * PAIR
            copies.append(
                pltpu.make_async_copy(
                    ref.at[i],
                    rows.at[pl.ds(pl.multiple_of(place, PAIR), PAIR)],
                    row_sems.at[len(copies)],
                )
            )
    for copy in copies:
        copy.start()
    start()
    total[...] = jnp.zeros_like(total)
    for copy in copies:
        copy.wait()
    run()
    for chip in range(CHIPS):
        for ref, target in ((own, core), (other, 1 - core)):
            place = pl.multiple_of((2 * chip + target) * ROWS, ROWS)
            ref[chip * ROWS : (chip + 1) * ROWS, :] = total[pl.ds(place, ROWS), :].astype(BF16)


def forward_sums(meta, coords, values, parts, dest_rows):
    slots = values.shape[0]
    source_rows = NZ * PAIR
    smem = pl.BlockSpec(memory_space=pltpu.SMEM)
    anywhere = pl.BlockSpec(memory_space=pl.ANY)
    vmem = pl.BlockSpec(memory_space=pltpu.VMEM)
    half = jax.ShapeDtypeStruct((dest_rows // 2, WIDTH), BF16)
    return pl.pallas_call(
        forward_kernel,
        out_shape=(half, half),
        in_specs=[smem, smem, pl.BlockSpec(memory_space=pltpu.HBM)] + [anywhere] * 5,
        out_specs=(vmem, vmem),
        scratch_shapes=[
            pltpu.VMEM(values.shape, BF16),
            pltpu.VMEM((source_rows, WIDTH), BF16),
            pltpu.VMEM((dest_rows, WIDTH), F32),
            pltpu.SemaphoreType.DMA((slots // GROUP,)),
            pltpu.SemaphoreType.DMA((NZ,)),
        ],
        compiler_params=pltpu.CompilerParams(vmem_limit_bytes=VMEM_LIMIT),
        name="forward_sums",
    )(meta, coords, values, *parts)


def middle_kernel(terms, weight, cotangent, act_ref, message):
    agg = jnp.sum(terms[...].astype(F32), axis=0).astype(BF16)
    w = weight[...]
    preact = jnp.dot(agg, w, preferred_element_type=F32)
    sigma = jax.nn.sigmoid(preact)
    act_ref[...] = (preact * sigma).astype(BF16)
    slope = sigma * (1.0 + preact * (1.0 - sigma))
    delta = (cotangent[...].astype(F32) * slope).astype(BF16)
    grad_agg = lax.dot_general(
        delta, w, (((1,), (1,)), ((), ())), preferred_element_type=F32
    ).astype(BF16)
    local = lax.dot_general(agg, delta, (((0,), (0,)), ((), ())), preferred_element_type=F32)
    share = WIDTH // N_SRC
    for chip in range(CHIPS):
        message[chip, :ROWS, :] = grad_agg
        message[chip, ROWS:, :] = local[2 * chip * share : 2 * (chip + 1) * share, :].astype(BF16)


def middle(terms, weight, cotangent):
    share = WIDTH // N_SRC
    vmem = pl.BlockSpec(memory_space=pltpu.VMEM)
    return pl.pallas_call(
        middle_kernel,
        out_shape=(
            jax.ShapeDtypeStruct((ROWS, WIDTH), BF16),
            jax.ShapeDtypeStruct((CHIPS, ROWS + 2 * share, WIDTH), BF16),
        ),
        in_specs=[vmem] * 3,
        out_specs=(vmem, vmem),
        compiler_params=pltpu.CompilerParams(vmem_limit_bytes=VMEM_LIMIT),
        name="middle",
    )(terms, weight, cotangent)


def backward_kernel(
    meta, coords, values_ref, mine, theirs, p0, p1, p3, p2a, p2b, wsum,
    held, rows, total, tail, value_sems, row_sems, tail_sems,
):
    slot_count, z, y, core = meta[0], meta[1], meta[2], meta[3]
    slots = values_ref.shape[0]

    def one_slot(ks):
        terms = [
            jnp.dot(held[k], block_of(rows, coords[slots + k]), preferred_element_type=F32)
            for k in ks
        ]
        for k, term in zip(ks, terms):
            add_block(total, coords[k], term)

    start, run = live_slots(slot_count, values_ref, held, value_sems, one_slot)
    share = (mine.shape[1] - ROWS) // 2
    copies = []
    for which, (ref, owner) in enumerate(((mine, core), (theirs, 1 - core))):
        for chip in range(CHIPS):
            place = pl.multiple_of((2 * chip + owner) * ROWS, ROWS)
            copies.append(
                pltpu.make_async_copy(
                    ref.at[chip, pl.ds(0, ROWS)], rows.at[pl.ds(place, ROWS)], row_sems.at[len(copies)]
                )
            )
        span = pl.ds(pl.multiple_of(ROWS + core * share, share), share)
        copies.append(pltpu.make_async_copy(ref.at[:, span], tail.at[which], tail_sems.at[which]))
    for copy in copies:
        copy.start()
    start()
    total[...] = jnp.zeros_like(total)
    for copy in copies:
        copy.wait()
    run()
    summed = jnp.sum(tail[...].astype(F32), axis=(0, 1))
    wsum[...] = summed
    for ref in (p1, p3, p2b):
        ref[ref.shape[0] - share :, :] = summed.astype(BF16)

    def put(ref, first_row, offset, member, other):
        place = (lax.rem(z + offset, 4) + 4 * member) * PAIR + (y if other == 0 else 1 - y) * ROWS
        chunk = total[pl.ds(pl.multiple_of(place, ROWS), ROWS), :]
        ref[first_row : first_row + ROWS, :] = chunk.astype(BF16)

    for other in range(2):
        for member in range(4):
            for ref, offset in ((p0, 0), (p1, 1), (p3, 3)):
                put(ref, (other * 4 + member) * ROWS, offset, member, other)
        for i in range(2):
            put(p2a, (other * 2 + i) * ROWS, 2, i, other)
            put(p2b, (other * 2 + i) * ROWS, 2, 2 + i, other)


def backward_sums(meta, coords, values, mine, theirs):
    slots = values.shape[0]
    share = (mine.shape[1] - ROWS) // 2
    dest_rows = N_SRC * ROWS
    source_rows = NZ * PAIR
    smem = pl.BlockSpec(memory_space=pltpu.SMEM)
    anywhere = pl.BlockSpec(memory_space=pl.ANY)
    vmem = pl.BlockSpec(memory_space=pltpu.VMEM)

    def rows_of(count):
        return jax.ShapeDtypeStruct((count, WIDTH), BF16)

    return pl.pallas_call(
        backward_kernel,
        out_shape=(
            rows_of(8 * ROWS),
            rows_of(8 * ROWS + share),
            rows_of(8 * ROWS + share),
            rows_of(4 * ROWS),
            rows_of(4 * ROWS + share),
            jax.ShapeDtypeStruct((share, WIDTH), F32),
        ),
        in_specs=[smem, smem, pl.BlockSpec(memory_space=pltpu.HBM), anywhere, anywhere],
        out_specs=(vmem,) * 6,
        scratch_shapes=[
            pltpu.VMEM(values.shape, BF16),
            pltpu.VMEM((dest_rows, WIDTH), BF16),
            pltpu.VMEM((source_rows, WIDTH), F32),
            pltpu.VMEM((2, CHIPS, share, WIDTH), BF16),
            pltpu.SemaphoreType.DMA((slots // GROUP,)),
            pltpu.SemaphoreType.DMA((N_SRC + 1,)),
            pltpu.SemaphoreType.DMA((2,)),
        ],
        compiler_params=pltpu.CompilerParams(vmem_limit_bytes=VMEM_LIMIT),
        name="backward_sums",
    )(meta, coords, values, mine, theirs)


def shift(array, step):
    return lax.ppermute(array, "dst", from_z(step))


def pair_swap(array, axis, groups, side):
    both = lax.all_gather(array, axis, axis=0, axis_index_groups=groups)
    return lax.dynamic_index_in_dim(both, 1 - side, 0, keepdims=False)


def gather_sources(features):
    own = lax.all_gather(features, "dst", axis=0, axis_index_groups=STRIDE_GROUPS)
    own = lax.all_gather(own, "dst", axis=1, tiled=True, axis_index_groups=Y_GROUPS)
    return own, shift(own, 1), shift(own[:2], 2), shift(own[2:], -2), shift(own, -1)


def scatter_sources(p0, p1, p3, p2a, p2b, wsum, y):
    half = 4 * ROWS
    quarter = half // 2
    below, above = shift(p1, -1), shift(p3, 1)
    low, high = shift(p2a, -2), shift(p2b, 2)
    w2 = wsum + below[2 * half :].astype(F32) + above[2 * half :].astype(F32) + high[half:].astype(F32)

    def side(first):
        far = jnp.concatenate([low[first // 2 : first // 2 + quarter], high[first // 2 : first // 2 + quarter]], 0)
        span = slice(first, first + half)
        near = below[span].astype(F32) + above[span].astype(F32)
        return p0[span].astype(F32) + near + far.astype(F32)

    sent = jnp.concatenate([side(half).astype(BF16), w2.astype(BF16)], 0)
    got = pair_swap(sent, "dst", Y_GROUPS, y).astype(F32)
    w3 = (w2 + got[half:]).astype(BF16)
    kept = (side(0) + got[:half]).astype(BF16).reshape(4, ROWS, WIDTH)
    message = jnp.concatenate([kept, jnp.broadcast_to(w3, (4,) + w3.shape)], 1)
    last = lax.all_to_all(message, "dst", 0, 0, tiled=True, axis_index_groups=STRIDE_GROUPS)
    last = jnp.sum(last.astype(F32), axis=0)
    return last[:ROWS].astype(BF16), last[ROWS:].astype(BF16)


def shards(features, weight, values, coords, counts, cotangent):
    tile_values = values[0, 0]
    pairs = coords[0, 0].T.reshape(-1)
    place = lax.axis_index("dst")
    z, y, core = place // NY, lax.rem(place, NY), lax.rem(lax.axis_index("src"), 2)
    meta = jnp.stack([counts[0, 0], z, y, core]).astype(jnp.int32)
    dest_rows = cotangent.shape[1] * N_SRC

    parts = gather_sources(features)
    own, other = forward_sums(meta, pairs, tile_values, parts, dest_rows)
    swapped = lax.ppermute(other, "src", CORE_SWAP)
    chip_sums = (own.astype(F32) + swapped.astype(F32)).astype(BF16)
    terms = lax.all_to_all(
        chip_sums.reshape(CHIPS, ROWS, WIDTH), "src", 0, 0, tiled=True, axis_index_groups=CORE_GROUPS
    )
    activations, message = middle(terms, weight, cotangent[0])
    mine = lax.all_to_all(message, "src", 0, 0, tiled=True, axis_index_groups=CORE_GROUPS)
    theirs = lax.ppermute(mine, "src", CORE_SWAP)
    sums = backward_sums(meta, pairs, tile_values, mine, theirs)
    input_grad, weight_part = scatter_sources(*sums, y)
    share = weight_part.shape[0]
    weight_part = jnp.broadcast_to(weight_part, (N_SRC, share, WIDTH))
    weight_grad = lax.all_to_all(weight_part, "src", 0, 0, tiled=True).reshape(WIDTH, WIDTH)
    return (activations[None], input_grad, weight_grad.astype(F32))


def solution(mesh):
    in_specs = (
        P(("src", "dst"), None),
        P(),
        P("src", "dst", None, None, None),
        P("src", "dst", None, None),
        P("src", "dst"),
        P("dst", "src", None),
    )
    out_specs = (P("dst", "src", None), P(("src", "dst"), None), P())
    return jax.shard_map(shards, mesh=mesh, in_specs=in_specs, out_specs=out_specs, check_vma=False)
```

```python
import functools

import jax
import jax.numpy as jnp
from jax import lax
from jax.experimental import pallas as pl
from jax.experimental.pallas import tpu as pltpu
from jax.sharding import PartitionSpec as P

BF16 = jnp.bfloat16
F32 = jnp.float32
NZ, NY = 16, 2
N_SRC = 16
SIDE = 128
WIDTH = 256
ROWS = 192
PAIR = NY * ROWS
VMEM_LIMIT = 32 * 1024 * 1024

STRIDE_GROUPS = [[2 * z + y for z in range(q, NZ, 4)] for q in range(4) for y in range(NY)]
Y_GROUPS = [[2 * z, 2 * z + 1] for z in range(NZ)]
Y_SWAP = [(d, d ^ 1) for d in range(NZ * NY)]
CHIPS = N_SRC // 2
CORE_GROUPS = [[2 * chip + core for chip in range(CHIPS)] for core in range(2)]
CORE_SWAP = [(s, s ^ 1) for s in range(N_SRC)]


def from_z(step):
    return [(((z + step) % NZ) * NY + y, z * NY + y) for z in range(NZ) for y in range(NY)]


def each_slot(slot_count, one_slot):
    def four(i, carry):
        one_slot([4 * i + u for u in range(4)])
        return carry

    def single(i, carry):
        one_slot([i])
        return carry

    lax.fori_loop(0, slot_count // 4, four, 0)
    lax.fori_loop((slot_count // 4) * 4, slot_count, single, 0)


def block_of(ref, index):
    return ref[pl.ds(pl.multiple_of(index * SIDE, SIDE), SIDE), :]


def add_block(ref, index, term):
    span = pl.ds(pl.multiple_of(index * SIDE, SIDE), SIDE)
    ref[span, :] = ref[span, :] + term


def forward_kernel(meta, coords, blocks, g0, g1, g2a, g2b, g3, own, other, rows, total):
    slot_count, z, core = meta[0], meta[1], meta[3]
    slots = blocks.shape[0]

    def one_slot(ks):
        terms = [
            lax.dot_general(
                blocks[k], block_of(rows, coords[k]), (((0,), (0,)), ((), ())), preferred_element_type=F32
            )
            for k in ks
        ]
        for k, term in zip(ks, terms):
            add_block(total, coords[slots + k], term)

    for offset, ref, first in ((0, g0, 0), (1, g1, 0), (3, g3, 0), (2, g2a, 0), (2, g2b, 2)):
        residue = lax.rem(z + offset, 4)
        for i in range(ref.shape[0]):
            place = pl.multiple_of((residue + 4 * (first + i)) * PAIR, PAIR)
            rows[pl.ds(place, PAIR), :] = ref[i]
    total[...] = jnp.zeros_like(total)
    each_slot(slot_count, one_slot)
    for chip in range(CHIPS):
        for ref, target in ((own, core), (other, 1 - core)):
            place = pl.multiple_of((2 * chip + target) * ROWS, ROWS)
            ref[chip * ROWS : (chip + 1) * ROWS, :] = total[pl.ds(place, ROWS), :].astype(BF16)


def forward_sums(meta, coords, values, parts, dest_rows):
    source_rows = NZ * PAIR
    smem = pl.BlockSpec(memory_space=pltpu.SMEM)
    vmem = pl.BlockSpec(memory_space=pltpu.VMEM)
    half = jax.ShapeDtypeStruct((dest_rows // 2, WIDTH), BF16)
    return pl.pallas_call(
        forward_kernel,
        out_shape=(half, half),
        in_specs=[smem, smem] + [vmem] * 6,
        out_specs=(vmem, vmem),
        scratch_shapes=[pltpu.VMEM((source_rows, WIDTH), BF16), pltpu.VMEM((dest_rows, WIDTH), F32)],
        compiler_params=pltpu.CompilerParams(vmem_limit_bytes=VMEM_LIMIT),
        name="forward_sums",
    )(meta, coords, values, *parts)


def middle_kernel(terms, weight, cotangent, act_ref, message):
    agg = jnp.sum(terms[...].astype(F32), axis=0).astype(BF16)
    w = weight[...]
    preact = jnp.dot(agg, w, preferred_element_type=F32)
    sigma = jax.nn.sigmoid(preact)
    act_ref[...] = (preact * sigma).astype(BF16)
    slope = sigma * (1.0 + preact * (1.0 - sigma))
    delta = (cotangent[...].astype(F32) * slope).astype(BF16)
    grad_agg = lax.dot_general(
        delta, w, (((1,), (1,)), ((), ())), preferred_element_type=F32
    ).astype(BF16)
    local = lax.dot_general(agg, delta, (((0,), (0,)), ((), ())), preferred_element_type=F32)
    share = WIDTH // N_SRC
    for chip in range(CHIPS):
        message[chip, :ROWS, :] = grad_agg
        message[chip, ROWS:, :] = local[2 * chip * share : 2 * (chip + 1) * share, :].astype(BF16)


def middle(terms, weight, cotangent):
    share = WIDTH // N_SRC
    vmem = pl.BlockSpec(memory_space=pltpu.VMEM)
    return pl.pallas_call(
        middle_kernel,
        out_shape=(
            jax.ShapeDtypeStruct((ROWS, WIDTH), BF16),
            jax.ShapeDtypeStruct((CHIPS, ROWS + 2 * share, WIDTH), BF16),
        ),
        in_specs=[vmem] * 3,
        out_specs=(vmem, vmem),
        compiler_params=pltpu.CompilerParams(vmem_limit_bytes=VMEM_LIMIT),
        name="middle",
    )(terms, weight, cotangent)


def backward_kernel(meta, coords, blocks, mine, theirs, *refs):
    kept, sent, (wsum, rows, total) = refs[:4], refs[4:8], refs[8:]
    slot_count, z, y, core = meta[0], meta[1], meta[2], meta[3]
    slots = blocks.shape[0]

    def one_slot(ks):
        terms = [
            jnp.dot(blocks[k], block_of(rows, coords[slots + k]), preferred_element_type=F32)
            for k in ks
        ]
        for k, term in zip(ks, terms):
            add_block(total, coords[k], term)

    share = wsum.shape[0]
    summed = jnp.zeros(wsum.shape, F32)
    for ref, owner in ((mine, core), (theirs, 1 - core)):
        for chip in range(CHIPS):
            place = pl.multiple_of((2 * chip + owner) * ROWS, ROWS)
            rows[pl.ds(place, ROWS), :] = ref[chip, :ROWS, :]
            tail = pl.ds(pl.multiple_of(ROWS + core * share, share), share)
            summed = summed + ref[chip, tail, :].astype(F32)
    wsum[...] = summed.astype(BF16)
    total[...] = jnp.zeros_like(total)
    each_slot(slot_count, one_slot)
    for refs, side in ((sent, 1 - y), (kept, y)):
        for offset, ref in zip((0, 1, 6, 15), refs):
            for member in range(4):
                place = lax.rem(z + offset + 4 * member, NZ) * PAIR + side * ROWS
                chunk = total[pl.ds(pl.multiple_of(place, ROWS), ROWS), :]
                ref[member * ROWS : (member + 1) * ROWS, :] = chunk.astype(BF16)


def backward_sums(meta, coords, values, mine, theirs):
    share = (mine.shape[1] - ROWS) // 2
    dest_rows = N_SRC * ROWS
    source_rows = NZ * PAIR
    smem = pl.BlockSpec(memory_space=pltpu.SMEM)
    vmem = pl.BlockSpec(memory_space=pltpu.VMEM)
    half = jax.ShapeDtypeStruct((4 * ROWS, WIDTH), BF16)
    out = pl.pallas_call(
        backward_kernel,
        out_shape=(half,) * 8 + (jax.ShapeDtypeStruct((share, WIDTH), BF16),),
        in_specs=[smem, smem, vmem, vmem, vmem],
        out_specs=(vmem,) * 9,
        scratch_shapes=[pltpu.VMEM((dest_rows, WIDTH), BF16), pltpu.VMEM((source_rows, WIDTH), F32)],
        compiler_params=pltpu.CompilerParams(vmem_limit_bytes=VMEM_LIMIT),
        name="backward_sums",
    )(meta, coords, values, mine, theirs)
    return out[:4], out[4:8], out[8]


def shift(array, step):
    return lax.ppermute(array, "dst", from_z(step))


def gather_sources(features):
    own = lax.all_gather(features, "dst", axis=0, axis_index_groups=STRIDE_GROUPS)
    own = lax.all_gather(own, "dst", axis=1, tiled=True, axis_index_groups=Y_GROUPS)
    right = shift(own, 1)
    left = shift(own, -1)
    return own, right, shift(right[:2], 1), shift(left[2:], -1), left


def total_of(*terms):
    return sum(term.astype(F32) for term in terms).astype(BF16)


def scatter_sources(kept, sent, weight_part):
    half = 2 * ROWS
    swapped = [None] * 4
    for which in (2, 1, 3, 0):
        swapped[which] = lax.ppermute(sent[which], "dst", Y_SWAP)
    low = shift(total_of(kept[2][:half], swapped[2][:half]), -1)
    high = shift(total_of(kept[2][half:], swapped[2][half:]), 1)
    none = jnp.zeros_like(low[:ROWS])
    up = total_of(kept[1], swapped[1], jnp.concatenate([none, low, none], 0))
    down = total_of(kept[3], swapped[3], jnp.concatenate([high, none, none], 0))
    near = total_of(kept[0], swapped[0], shift(up, -1), shift(down, 1)).reshape(4, ROWS, WIDTH)
    near, weight_part = lax.optimization_barrier((near, weight_part))
    return total_of(near[0], shift(near[2], -8), shift(near[1], -4), shift(near[3], 4)), weight_part


def everywhere(part, axis, count):
    copies = jnp.broadcast_to(part, (count,) + part.shape)
    return lax.all_to_all(copies, axis, 0, 0, tiled=True)


def shards(features, weight, values, coords, counts, cotangent):
    tile_values = values[0, 0]
    pairs = coords[0, 0].T.reshape(-1)
    place = lax.axis_index("dst")
    z, y, core = place // NY, lax.rem(place, NY), lax.rem(lax.axis_index("src"), 2)
    meta = jnp.stack([counts[0, 0], z, y, core]).astype(jnp.int32)
    dest_rows = cotangent.shape[1] * N_SRC

    parts = gather_sources(features)
    own, other = forward_sums(meta, pairs, tile_values, parts, dest_rows)
    swapped = lax.ppermute(other, "src", CORE_SWAP)
    chip_sums = (own.astype(F32) + swapped.astype(F32)).astype(BF16)
    terms = lax.all_to_all(
        chip_sums.reshape(CHIPS, ROWS, WIDTH), "src", 0, 0, tiled=True, axis_index_groups=CORE_GROUPS
    )
    activations, message = middle(terms, weight, cotangent[0])
    mine = lax.all_to_all(message, "src", 0, 0, tiled=True, axis_index_groups=CORE_GROUPS)
    theirs = lax.ppermute(mine, "src", CORE_SWAP)
    kept, sent, weight_part = backward_sums(meta, pairs, tile_values, mine, theirs)
    input_grad, weight_part = scatter_sources(kept, sent, weight_part)
    weight_part = everywhere(weight_part, "dst", NZ * NY)
    weight_part = jnp.sum(weight_part.astype(F32), axis=0).astype(BF16)
    weight_grad = everywhere(weight_part, "src", N_SRC).reshape(WIDTH, WIDTH)
    return (activations[None], input_grad, weight_grad.astype(F32))


def solution(mesh):
    in_specs = (
        P(("src", "dst"), None),
        P(),
        P("src", "dst", None, None, None),
        P("src", "dst", None, None),
        P("src", "dst"),
        P("dst", "src", None),
    )
    out_specs = (P("dst", "src", None), P(("src", "dst"), None), P())
    return jax.shard_map(shards, mesh=mesh, in_specs=in_specs, out_specs=out_specs, check_vma=False)
```

```python
import functools

import jax
import jax.numpy as jnp
from jax import lax
from jax.experimental import pallas as pl
from jax.experimental.pallas import tpu as pltpu
from jax.sharding import PartitionSpec as P

BF16 = jnp.bfloat16
F32 = jnp.float32
NZ, NY = 16, 2
N_SRC = 16
SIDE = 128
WIDTH = 256
ROWS = 192
PAIR = NY * ROWS
VMEM_LIMIT = 24 * 1024 * 1024

STRIDE_GROUPS = [[2 * z + y for z in range(q, NZ, 4)] for q in range(4) for y in range(NY)]
Y_GROUPS = [[2 * z, 2 * z + 1] for z in range(NZ)]
Y_SWAP = [(d, d ^ 1) for d in range(NZ * NY)]
CHIPS = N_SRC // 2
CORE_GROUPS = [[2 * chip + core for chip in range(CHIPS)] for core in range(2)]
CHIP_PAIRS = [[2 * chip, 2 * chip + 1] for chip in range(CHIPS)]
PEER_GROUPS = [
    [(2 * chip + core) * NZ * NY + (q + 4 * m) * NY + y for m in range(4) for chip in range(CHIPS)]
    for core in range(2)
    for q in range(4)
    for y in range(NY)
]
CORE_SWAP = [(s, s ^ 1) for s in range(N_SRC)]


def from_z(step):
    return [(((z + step) % NZ) * NY + y, z * NY + y) for z in range(NZ) for y in range(NY)]


def each_slot(slot_count, one_slot):
    done = 0
    for step in (16, 4, 1):

        def several(i, carry, step=step, done=done):
            one_slot([done + i * step + u for u in range(step)])
            return carry

        turns = (slot_count - done) // step
        lax.fori_loop(0, turns, several, 0)
        done = done + turns * step


def block_of(ref, index):
    return ref[pl.ds(pl.multiple_of(index * SIDE, SIDE), SIDE), :]


def add_block(ref, index, term):
    span = pl.ds(pl.multiple_of(index * SIDE, SIDE), SIDE)
    ref[span, :] = ref[span, :] + term


def forward_kernel(meta, coords, blocks, g0, g1a, g1b, g2a, g2b, g3a, g3b, own, other, rows, total):
    slot_count, z, core = meta[0], meta[1], meta[3]
    slots = blocks.shape[0]

    def one_slot(ks):
        terms = [
            lax.dot_general(
                blocks[k], block_of(rows, coords[k]), (((0,), (0,)), ((), ())), preferred_element_type=F32
            )
            for k in ks
        ]
        for k, term in zip(ks, terms):
            add_block(total, coords[slots + k], term)

    pieces = ((0, g0, 0), (1, g1a, 0), (1, g1b, 2), (2, g2a, 0), (2, g2b, 2), (3, g3a, 0), (3, g3b, 2))
    for offset, ref, first in pieces:
        residue = lax.rem(z + offset, 4)
        for i in range(ref.shape[0]):
            place = pl.multiple_of((residue + 4 * (first + i)) * PAIR, PAIR)
            rows[pl.ds(place, PAIR), :] = ref[i]
    total[...] = jnp.zeros_like(total)
    each_slot(slot_count, one_slot)
    for chip in range(CHIPS):
        for ref, target in ((own, core), (other, 1 - core)):
            place = pl.multiple_of((2 * chip + target) * ROWS, ROWS)
            ref[chip * ROWS : (chip + 1) * ROWS, :] = total[pl.ds(place, ROWS), :].astype(BF16)


def forward_sums(meta, coords, values, parts, dest_rows):
    source_rows = NZ * PAIR
    smem = pl.BlockSpec(memory_space=pltpu.SMEM)
    vmem = pl.BlockSpec(memory_space=pltpu.VMEM)
    half = jax.ShapeDtypeStruct((dest_rows // 2, WIDTH), BF16)
    return pl.pallas_call(
        forward_kernel,
        out_shape=(half, half),
        in_specs=[smem, smem] + [vmem] * 8,
        out_specs=(vmem, vmem),
        scratch_shapes=[pltpu.VMEM((source_rows, WIDTH), BF16), pltpu.VMEM((dest_rows, WIDTH), F32)],
        compiler_params=pltpu.CompilerParams(vmem_limit_bytes=VMEM_LIMIT),
        name="forward_sums",
    )(meta, coords, values, *parts)


def middle_kernel(terms, weight, cotangent, act_ref, message):
    agg = jnp.sum(terms[...].astype(F32), axis=0).astype(BF16)
    w = weight[...]
    preact = jnp.dot(agg, w, preferred_element_type=F32)
    sigma = jax.nn.sigmoid(preact)
    act_ref[...] = (preact * sigma).astype(BF16)
    slope = sigma * (1.0 + preact * (1.0 - sigma))
    delta = (cotangent[...].astype(F32) * slope).astype(BF16)
    grad_agg = lax.dot_general(
        delta, w, (((1,), (1,)), ((), ())), preferred_element_type=F32
    ).astype(BF16)
    local = lax.dot_general(agg, delta, (((0,), (0,)), ((), ())), preferred_element_type=F32)
    share = WIDTH // N_SRC
    for chip in range(CHIPS):
        message[chip, :ROWS, :] = grad_agg
        message[chip, ROWS:, :] = local[2 * chip * share : 2 * (chip + 1) * share, :].astype(BF16)


def middle(terms, weight, cotangent):
    share = WIDTH // N_SRC
    vmem = pl.BlockSpec(memory_space=pltpu.VMEM)
    return pl.pallas_call(
        middle_kernel,
        out_shape=(
            jax.ShapeDtypeStruct((ROWS, WIDTH), BF16),
            jax.ShapeDtypeStruct((CHIPS, ROWS + 2 * share, WIDTH), BF16),
        ),
        in_specs=[vmem] * 3,
        out_specs=(vmem, vmem),
        compiler_params=pltpu.CompilerParams(vmem_limit_bytes=VMEM_LIMIT),
        name="middle",
    )(terms, weight, cotangent)


def backward_kernel(meta, coords, blocks, mine, theirs, *refs):
    kept, sent, (wsum, rows, total) = refs[:4], refs[4:8], refs[8:]
    slot_count, z, y, core = meta[0], meta[1], meta[2], meta[3]
    slots = blocks.shape[0]

    def one_slot(ks):
        terms = [
            jnp.dot(blocks[k], block_of(rows, coords[slots + k]), preferred_element_type=F32)
            for k in ks
        ]
        for k, term in zip(ks, terms):
            add_block(total, coords[k], term)

    share = wsum.shape[0]
    summed = jnp.zeros(wsum.shape, F32)
    for ref, owner in ((mine, core), (theirs, 1 - core)):
        for chip in range(CHIPS):
            place = pl.multiple_of((2 * chip + owner) * ROWS, ROWS)
            rows[pl.ds(place, ROWS), :] = ref[chip, :ROWS, :]
            tail = pl.ds(pl.multiple_of(ROWS + core * share, share), share)
            summed = summed + ref[chip, tail, :].astype(F32)
    wsum[...] = summed
    sent[2][4 * ROWS :, :] = summed.astype(BF16)
    total[...] = jnp.zeros_like(total)
    each_slot(slot_count, one_slot)
    for refs, side in ((sent, 1 - y), (kept, y)):
        for offset, ref in zip((0, 1, 6, 15), refs):
            for member in range(4):
                place = lax.rem(z + offset + 4 * member, NZ) * PAIR + side * ROWS
                chunk = total[pl.ds(pl.multiple_of(place, ROWS), ROWS), :]
                ref[member * ROWS : (member + 1) * ROWS, :] = chunk.astype(BF16)


def backward_sums(meta, coords, values, mine, theirs):
    share = (mine.shape[1] - ROWS) // 2
    dest_rows = N_SRC * ROWS
    source_rows = NZ * PAIR
    smem = pl.BlockSpec(memory_space=pltpu.SMEM)
    vmem = pl.BlockSpec(memory_space=pltpu.VMEM)
    half = jax.ShapeDtypeStruct((4 * ROWS, WIDTH), BF16)
    out = pl.pallas_call(
        backward_kernel,
        out_shape=(half,) * 6
        + (
            jax.ShapeDtypeStruct((4 * ROWS + share, WIDTH), BF16),
            half,
            jax.ShapeDtypeStruct((share, WIDTH), F32),
        ),
        in_specs=[smem, smem, vmem, vmem, vmem],
        out_specs=(vmem,) * 9,
        scratch_shapes=[pltpu.VMEM((dest_rows, WIDTH), BF16), pltpu.VMEM((source_rows, WIDTH), F32)],
        compiler_params=pltpu.CompilerParams(vmem_limit_bytes=VMEM_LIMIT),
        name="backward_sums",
    )(meta, coords, values, mine, theirs)
    return out[:4], out[4:8], out[8]


def shift(array, step):
    return lax.ppermute(array, "dst", from_z(step))


def gather_sources(features):
    own = lax.all_gather(features, "dst", axis=0, axis_index_groups=STRIDE_GROUPS)
    own = lax.all_gather(own, "dst", axis=1, tiled=True, axis_index_groups=Y_GROUPS)
    low, high = own[:2], own[2:]
    right_low, left_high = shift(low, 1), shift(high, -1)
    right_high, left_low = shift(high, 1), shift(low, -1)
    far_low, far_high = shift(right_low, 1), shift(left_high, -1)
    return own, right_low, right_high, far_low, far_high, left_low, left_high


def total_of(*terms):
    return sum(term.astype(F32) for term in terms).astype(BF16)


def total_f32(*terms):
    return sum(term.astype(F32) for term in terms)


def scatter_sources(kept, sent, weight_part):
    half, full = 2 * ROWS, 4 * ROWS
    swapped = [None] * 4
    for which in (2, 1, 3, 0):
        swapped[which] = lax.ppermute(sent[which], "dst", Y_SWAP)
    w = total_f32(weight_part, swapped[2][full:])
    low = shift(total_of(kept[2][:half], swapped[2][:half]), -1)
    high = jnp.concatenate([total_of(kept[2][half:], swapped[2][half:full]), w.astype(BF16)], 0)
    high = shift(high, 1)
    w = total_of(w, high[half:])
    none = jnp.zeros_like(low[:ROWS])
    up = total_of(kept[1], swapped[1], jnp.concatenate([none, low, none], 0))
    down = total_of(kept[3], swapped[3], jnp.concatenate([high[:half], none, none], 0))
    up = shift(jnp.concatenate([up, w], 0), -1)
    down = shift(jnp.concatenate([down, w], 0), 1)
    w = total_of(up[full:], down[full:])
    near = total_of(kept[0], swapped[0], up[:full], down[:full]).reshape(4, ROWS, WIDTH)
    far, left, right = shift(near[2], -8), shift(near[1], -4), shift(near[3], 4)
    weight_grad, mine = lax.optimization_barrier((gather_weight(w), near[0]))
    return total_of(mine, far, left, right), weight_grad


def gather_weight(part):
    share = part.shape[0]
    pair = lax.all_gather(part, "src", axis=0, tiled=True, axis_index_groups=CHIP_PAIRS)
    copies = jnp.broadcast_to(pair, (4 * CHIPS,) + pair.shape)
    pieces = lax.all_to_all(copies, ("src", "dst"), 0, 0, tiled=True, axis_index_groups=PEER_GROUPS)
    return jnp.sum(pieces.astype(F32).reshape(4, CHIPS * 2 * share, WIDTH), axis=0)


def shards(features, weight, values, coords, counts, cotangent):
    tile_values = values[0, 0]
    pairs = coords[0, 0].T.reshape(-1)
    place = lax.axis_index("dst")
    z, y, core = place // NY, lax.rem(place, NY), lax.rem(lax.axis_index("src"), 2)
    meta = jnp.stack([counts[0, 0], z, y, core]).astype(jnp.int32)
    dest_rows = cotangent.shape[1] * N_SRC

    parts = gather_sources(features)
    tile_values, _ = lax.optimization_barrier((tile_values, parts[0]))
    live = jnp.arange(tile_values.shape[0], dtype=jnp.int32) < meta[0]
    blocks = jnp.where(live[:, None, None], tile_values, jnp.zeros((), BF16))
    own, other = forward_sums(meta, pairs, blocks, parts, dest_rows)
    swapped = lax.ppermute(other, "src", CORE_SWAP)
    chip_sums = (own.astype(F32) + swapped.astype(F32)).astype(BF16)
    terms = lax.all_to_all(
        chip_sums.reshape(CHIPS, ROWS, WIDTH), "src", 0, 0, tiled=True, axis_index_groups=CORE_GROUPS
    )
    activations, message = middle(terms, weight, cotangent[0])
    mine = lax.all_to_all(message, "src", 0, 0, tiled=True, axis_index_groups=CORE_GROUPS)
    theirs = lax.ppermute(mine, "src", CORE_SWAP)
    kept, sent, weight_part = backward_sums(meta, pairs, blocks, mine, theirs)
    input_grad, weight_grad = scatter_sources(kept, sent, weight_part)
    return (activations[None], input_grad, weight_grad)


def solution(mesh):
    in_specs = (
        P(("src", "dst"), None),
        P(),
        P("src", "dst", None, None, None),
        P("src", "dst", None, None),
        P("src", "dst"),
        P("dst", "src", None),
    )
    out_specs = (P("dst", "src", None), P(("src", "dst"), None), P())
    return jax.shard_map(shards, mesh=mesh, in_specs=in_specs, out_specs=out_specs, check_vma=False)
```

```python
import functools

import jax
import jax.numpy as jnp
from jax import lax
from jax.experimental import pallas as pl
from jax.experimental.pallas import tpu as pltpu
from jax.sharding import PartitionSpec as P

BF16 = jnp.bfloat16
F32 = jnp.float32
NZ, NY = 16, 2
N_SRC = 16
SIDE = 128
WIDTH = 256
ROWS = 192
PAIR = NY * ROWS
VMEM_LIMIT = 24 * 1024 * 1024

STRIDE_GROUPS = [[2 * z + y for z in range(q, NZ, 4)] for q in range(4) for y in range(NY)]
Y_GROUPS = [[2 * z, 2 * z + 1] for z in range(NZ)]
Y_SWAP = [(d, d ^ 1) for d in range(NZ * NY)]
CHIPS = N_SRC // 2
CORE_GROUPS = [[2 * chip + core for chip in range(CHIPS)] for core in range(2)]
CORE_SWAP = [(s, s ^ 1) for s in range(N_SRC)]


def from_z(step):
    return [(((z + step) % NZ) * NY + y, z * NY + y) for z in range(NZ) for y in range(NY)]


def each_slot(slot_count, one_slot):
    done = 0
    for step in (16, 4, 1):

        def several(i, carry, step=step, done=done):
            one_slot([done + i * step + u for u in range(step)])
            return carry

        turns = (slot_count - done) // step
        lax.fori_loop(0, turns, several, 0)
        done = done + turns * step


def block_of(ref, index):
    return ref[pl.ds(pl.multiple_of(index * SIDE, SIDE), SIDE), :]


def add_block(ref, index, term):
    span = pl.ds(pl.multiple_of(index * SIDE, SIDE), SIDE)
    ref[span, :] = ref[span, :] + term


def forward_kernel(meta, coords, blocks, g0, g1a, g1b, g2a, g2b, g3a, g3b, own, other, rows, total):
    slot_count, z, core = meta[0], meta[1], meta[3]
    slots = blocks.shape[0]

    def one_slot(ks):
        terms = [
            lax.dot_general(
                blocks[k], block_of(rows, coords[k]), (((0,), (0,)), ((), ())), preferred_element_type=F32
            )
            for k in ks
        ]
        for k, term in zip(ks, terms):
            add_block(total, coords[slots + k], term)

    pieces = ((0, g0, 0), (1, g1a, 0), (1, g1b, 2), (2, g2a, 0), (2, g2b, 2), (3, g3a, 0), (3, g3b, 2))
    for offset, ref, first in pieces:
        residue = lax.rem(z + offset, 4)
        for i in range(ref.shape[0]):
            place = pl.multiple_of((residue + 4 * (first + i)) * PAIR, PAIR)
            rows[pl.ds(place, PAIR), :] = ref[i]
    total[...] = jnp.zeros_like(total)
    each_slot(slot_count, one_slot)
    for chip in range(CHIPS):
        for ref, target in ((own, core), (other, 1 - core)):
            place = pl.multiple_of((2 * chip + target) * ROWS, ROWS)
            ref[chip * ROWS : (chip + 1) * ROWS, :] = total[pl.ds(place, ROWS), :].astype(BF16)


def forward_sums(meta, coords, values, parts, dest_rows):
    source_rows = NZ * PAIR
    smem = pl.BlockSpec(memory_space=pltpu.SMEM)
    vmem = pl.BlockSpec(memory_space=pltpu.VMEM)
    half = jax.ShapeDtypeStruct((dest_rows // 2, WIDTH), BF16)
    return pl.pallas_call(
        forward_kernel,
        out_shape=(half, half),
        in_specs=[smem, smem] + [vmem] * 8,
        out_specs=(vmem, vmem),
        scratch_shapes=[pltpu.VMEM((source_rows, WIDTH), BF16), pltpu.VMEM((dest_rows, WIDTH), F32)],
        compiler_params=pltpu.CompilerParams(vmem_limit_bytes=VMEM_LIMIT),
        name="forward_sums",
    )(meta, coords, values, *parts)


def middle_kernel(terms, weight, cotangent, act_ref, message):
    agg = jnp.sum(terms[...].astype(F32), axis=0).astype(BF16)
    w = weight[...]
    preact = jnp.dot(agg, w, preferred_element_type=F32)
    sigma = jax.nn.sigmoid(preact)
    act_ref[...] = (preact * sigma).astype(BF16)
    slope = sigma * (1.0 + preact * (1.0 - sigma))
    delta = (cotangent[...].astype(F32) * slope).astype(BF16)
    grad_agg = lax.dot_general(
        delta, w, (((1,), (1,)), ((), ())), preferred_element_type=F32
    ).astype(BF16)
    local = lax.dot_general(agg, delta, (((0,), (0,)), ((), ())), preferred_element_type=F32)
    share = WIDTH // N_SRC
    for chip in range(CHIPS):
        message[chip, :ROWS, :] = grad_agg
        message[chip, ROWS:, :] = local[2 * chip * share : 2 * (chip + 1) * share, :].astype(BF16)


def middle(terms, weight, cotangent):
    share = WIDTH // N_SRC
    vmem = pl.BlockSpec(memory_space=pltpu.VMEM)
    return pl.pallas_call(
        middle_kernel,
        out_shape=(
            jax.ShapeDtypeStruct((ROWS, WIDTH), BF16),
            jax.ShapeDtypeStruct((CHIPS, ROWS + 2 * share, WIDTH), BF16),
        ),
        in_specs=[vmem] * 3,
        out_specs=(vmem, vmem),
        compiler_params=pltpu.CompilerParams(vmem_limit_bytes=VMEM_LIMIT),
        name="middle",
    )(terms, weight, cotangent)


def backward_kernel(
    meta, coords, blocks, mine, theirs, kept0, kept1, kept2, kept3, sent0, sent13, sent2, wsum, rows, total
):
    slot_count, z, y, core = meta[0], meta[1], meta[2], meta[3]
    slots = blocks.shape[0]

    def one_slot(ks):
        terms = [
            jnp.dot(blocks[k], block_of(rows, coords[slots + k]), preferred_element_type=F32)
            for k in ks
        ]
        for k, term in zip(ks, terms):
            add_block(total, coords[k], term)

    share = wsum.shape[0]
    summed = jnp.zeros(wsum.shape, F32)
    for ref, owner in ((mine, core), (theirs, 1 - core)):
        for chip in range(CHIPS):
            place = pl.multiple_of((2 * chip + owner) * ROWS, ROWS)
            rows[pl.ds(place, ROWS), :] = ref[chip, :ROWS, :]
            tail = pl.ds(pl.multiple_of(ROWS + core * share, share), share)
            summed = summed + ref[chip, tail, :].astype(F32)
    wsum[...] = summed
    sent2[4 * ROWS :, :] = summed.astype(BF16)
    total[...] = jnp.zeros_like(total)
    each_slot(slot_count, one_slot)
    mirror = 1 - y
    lists = (
        (sent2, 0, 6, mirror), (sent13, 0, 1, mirror), (sent13, 4, 15, mirror), (sent0, 0, 0, mirror),
        (kept0, 0, 0, y), (kept1, 0, 1, y), (kept2, 0, 6, y), (kept3, 0, 15, y),
    )
    for ref, first, offset, side in lists:
        for member in range(4):
            place = lax.rem(z + offset + 4 * member, NZ) * PAIR + side * ROWS
            chunk = total[pl.ds(pl.multiple_of(place, ROWS), ROWS), :]
            ref[(first + member) * ROWS : (first + member + 1) * ROWS, :] = chunk.astype(BF16)


def backward_sums(meta, coords, values, mine, theirs):
    share = (mine.shape[1] - ROWS) // 2
    dest_rows = N_SRC * ROWS
    source_rows = NZ * PAIR
    smem = pl.BlockSpec(memory_space=pltpu.SMEM)
    vmem = pl.BlockSpec(memory_space=pltpu.VMEM)

    def rows_of(count):
        return jax.ShapeDtypeStruct((count, WIDTH), BF16)

    list_rows = 4 * ROWS
    out = pl.pallas_call(
        backward_kernel,
        out_shape=(rows_of(list_rows),) * 5
        + (rows_of(2 * list_rows), rows_of(list_rows + share), jax.ShapeDtypeStruct((share, WIDTH), F32)),
        in_specs=[smem, smem, vmem, vmem, vmem],
        out_specs=(vmem,) * 8,
        scratch_shapes=[pltpu.VMEM((dest_rows, WIDTH), BF16), pltpu.VMEM((source_rows, WIDTH), F32)],
        compiler_params=pltpu.CompilerParams(vmem_limit_bytes=VMEM_LIMIT),
        name="backward_sums",
    )(meta, coords, values, mine, theirs)
    return (out[:4],) + tuple(out[4:])


def shift(array, step):
    return lax.ppermute(array, "dst", from_z(step))


def gather_sources(features):
    own = lax.all_gather(features, "dst", axis=0, axis_index_groups=STRIDE_GROUPS)
    own = lax.all_gather(own, "dst", axis=1, tiled=True, axis_index_groups=Y_GROUPS)
    low, high = own[:2], own[2:]
    right_low, left_high = shift(low, 1), shift(high, -1)
    right_high, left_low = shift(high, 1), shift(low, -1)
    far_low, far_high = shift(right_low, 1), shift(left_high, -1)
    return own, right_low, right_high, far_low, far_high, left_low, left_high


def total_of(*terms):
    return sum(term.astype(F32) for term in terms).astype(BF16)


def total_f32(*terms):
    return sum(term.astype(F32) for term in terms)


def total_f32(*terms):
    return sum(term.astype(F32) for term in terms)


def pair_swap(array, axis, groups, side):
    both = lax.all_gather(array, axis, axis=0, axis_index_groups=groups)
    return lax.dynamic_index_in_dim(both, 1 - side, 0, keepdims=False)


def scatter_sources(kept, sent0, sent13, sent2, w, y):
    half, full = 2 * ROWS, 4 * ROWS
    swap2 = pair_swap(sent2, "dst", Y_GROUPS, y)
    swap13 = lax.ppermute(sent13, "dst", Y_SWAP)
    w = total_f32(w, swap2[full:])
    low = shift(total_of(kept[2][:half], swap2[:half]), -1)
    high = jnp.concatenate([total_of(kept[2][half:], swap2[half:full]), w.astype(BF16)], 0)
    high = shift(high, 1)
    sent0, low = lax.optimization_barrier((sent0, low))
    swap0 = lax.ppermute(sent0, "dst", Y_SWAP)
    w = total_of(w, high[half:])
    none = jnp.zeros_like(low[:ROWS])
    up = total_of(kept[1], swap13[:full], jnp.concatenate([none, low, none], 0))
    down = total_of(kept[3], swap13[full:], jnp.concatenate([high[:half], none, none], 0))
    up = shift(jnp.concatenate([up, w], 0), -1)
    down = shift(jnp.concatenate([down, w], 0), 1)
    w = total_of(up[full:], down[full:])
    near = total_of(kept[0], swap0, up[:full], down[:full]).reshape(4, ROWS, WIDTH)

    part = ROWS // 2
    from_left = shift(jnp.concatenate([near[2, :part], w], 0), -4)
    from_right = shift(jnp.concatenate([near[2, part:], w], 0), 4)
    w_left, w_right = from_left[part:], from_right[part:]
    none = jnp.zeros((part, WIDTH), BF16)
    left = shift(total_of(near[1], jnp.concatenate([from_left[:part], none], 0)), -4)
    right = total_of(near[3], jnp.concatenate([none, from_right[:part]], 0))
    right = shift(jnp.concatenate([right, w_right], 0), 4)
    w = total_of(w, w_left, w_right, right[ROWS:])
    return total_of(near[0], left, right[:ROWS]), w


def gather_weight(part):
    copies = jnp.broadcast_to(part, (N_SRC,) + part.shape)
    return lax.all_to_all(copies, "src", 0, 0, tiled=True).reshape(WIDTH, WIDTH).astype(F32)


def shards(features, weight, values, coords, counts, cotangent):
    tile_values = values[0, 0]
    pairs = coords[0, 0].T.reshape(-1)
    place = lax.axis_index("dst")
    z, y, core = place // NY, lax.rem(place, NY), lax.rem(lax.axis_index("src"), 2)
    meta = jnp.stack([counts[0, 0], z, y, core]).astype(jnp.int32)
    dest_rows = cotangent.shape[1] * N_SRC

    parts = gather_sources(features)
    tile_values, _ = lax.optimization_barrier((tile_values, parts[0]))
    live = jnp.arange(tile_values.shape[0], dtype=jnp.int32) < meta[0]
    blocks = jnp.where(live[:, None, None], tile_values, jnp.zeros((), BF16))
    own, other = forward_sums(meta, pairs, blocks, parts, dest_rows)
    swapped = lax.ppermute(other, "src", CORE_SWAP)
    chip_sums = (own.astype(F32) + swapped.astype(F32)).astype(BF16)
    terms = lax.all_to_all(
        chip_sums.reshape(CHIPS, ROWS, WIDTH), "src", 0, 0, tiled=True, axis_index_groups=CORE_GROUPS
    )
    activations, message = middle(terms, weight, cotangent[0])
    mine = lax.all_to_all(message, "src", 0, 0, tiled=True, axis_index_groups=CORE_GROUPS)
    theirs = lax.ppermute(mine, "src", CORE_SWAP)
    sums = backward_sums(meta, pairs, blocks, mine, theirs)
    input_grad, weight_part = scatter_sources(*sums, y)
    weight_grad = gather_weight(weight_part)
    return (activations[None], input_grad, weight_grad)


def solution(mesh):
    in_specs = (
        P(("src", "dst"), None),
        P(),
        P("src", "dst", None, None, None),
        P("src", "dst", None, None),
        P("src", "dst"),
        P("dst", "src", None),
    )
    out_specs = (P("dst", "src", None), P(("src", "dst"), None), P())
    return jax.shard_map(shards, mesh=mesh, in_specs=in_specs, out_specs=out_specs, check_vma=False)
```

```python
import functools

import jax
import jax.numpy as jnp
from jax import lax
from jax.experimental import pallas as pl
from jax.experimental.pallas import tpu as pltpu
from jax.sharding import PartitionSpec as P

BF16 = jnp.bfloat16
F32 = jnp.float32
NZ, NY = 16, 2
N_SRC = 16
SIDE = 128
WIDTH = 256
ROWS = 192
PAIR = NY * ROWS
VMEM_LIMIT = 24 * 1024 * 1024

STRIDE_GROUPS = [[2 * z + y for z in range(q, NZ, 4)] for q in range(4) for y in range(NY)]
Y_GROUPS = [[2 * z, 2 * z + 1] for z in range(NZ)]
Y_SWAP = [(d, d ^ 1) for d in range(NZ * NY)]
CHIPS = N_SRC // 2
CORE_GROUPS = [[2 * chip + core for chip in range(CHIPS)] for core in range(2)]
CORE_SWAP = [(s, s ^ 1) for s in range(N_SRC)]


def from_z(step):
    return [(((z + step) % NZ) * NY + y, z * NY + y) for z in range(NZ) for y in range(NY)]


def each_slot(slot_count, one_slot):
    done = 0
    for step in (36, 12, 4, 1):

        def several(i, carry, step=step, done=done):
            one_slot([done + i * step + u for u in range(step)])
            return carry

        turns = (slot_count - done) // step
        lax.fori_loop(0, turns, several, 0)
        done = done + turns * step


def block_of(ref, index):
    return ref[pl.ds(pl.multiple_of(index * SIDE, SIDE), SIDE), :]


def add_block(ref, index, term):
    span = pl.ds(pl.multiple_of(index * SIDE, SIDE), SIDE)
    ref[span, :] = ref[span, :] + term


def forward_kernel(meta, coords, blocks, g0, g1a, g1b, g2a, g2b, g3a, g3b, own, other, rows, total):
    slot_count, z, core = meta[0], meta[1], meta[3]
    slots = blocks.shape[0]

    def one_slot(ks):
        terms = [
            lax.dot_general(
                blocks[k], block_of(rows, coords[k]), (((0,), (0,)), ((), ())), preferred_element_type=F32
            )
            for k in ks
        ]
        for k, term in zip(ks, terms):
            add_block(total, coords[slots + k], term)

    pieces = ((0, g0, 0), (1, g1a, 0), (1, g1b, 2), (2, g2a, 0), (2, g2b, 2), (3, g3a, 0), (3, g3b, 2))
    for offset, ref, first in pieces:
        residue = lax.rem(z + offset, 4)
        for i in range(ref.shape[0]):
            place = pl.multiple_of((residue + 4 * (first + i)) * PAIR, PAIR)
            rows[pl.ds(place, PAIR), :] = ref[i]
    total[...] = jnp.zeros_like(total)
    each_slot(slot_count, one_slot)
    for chip in range(CHIPS):
        for ref, target in ((own, core), (other, 1 - core)):
            place = pl.multiple_of((2 * chip + target) * ROWS, ROWS)
            ref[chip * ROWS : (chip + 1) * ROWS, :] = total[pl.ds(place, ROWS), :].astype(BF16)


def forward_sums(meta, coords, values, parts, dest_rows):
    source_rows = NZ * PAIR
    smem = pl.BlockSpec(memory_space=pltpu.SMEM)
    vmem = pl.BlockSpec(memory_space=pltpu.VMEM)
    half = jax.ShapeDtypeStruct((dest_rows // 2, WIDTH), BF16)
    return pl.pallas_call(
        forward_kernel,
        out_shape=(half, half),
        in_specs=[smem, smem] + [vmem] * 8,
        out_specs=(vmem, vmem),
        scratch_shapes=[pltpu.VMEM((source_rows, WIDTH), BF16), pltpu.VMEM((dest_rows, WIDTH), F32)],
        compiler_params=pltpu.CompilerParams(vmem_limit_bytes=VMEM_LIMIT),
        name="forward_sums",
    )(meta, coords, values, *parts)


def middle_kernel(terms, weight, cotangent, act_ref, message):
    agg = jnp.sum(terms[...].astype(F32), axis=0).astype(BF16)
    w = weight[...]
    preact = jnp.dot(agg, w, preferred_element_type=F32)
    sigma = jax.nn.sigmoid(preact)
    act_ref[...] = (preact * sigma).astype(BF16)
    slope = sigma * (1.0 + preact * (1.0 - sigma))
    delta = (cotangent[...].astype(F32) * slope).astype(BF16)
    grad_agg = lax.dot_general(
        delta, w, (((1,), (1,)), ((), ())), preferred_element_type=F32
    ).astype(BF16)
    local = lax.dot_general(agg, delta, (((0,), (0,)), ((), ())), preferred_element_type=F32)
    share = WIDTH // N_SRC
    for chip in range(CHIPS):
        message[chip, :ROWS, :] = grad_agg
        message[chip, ROWS:, :] = local[2 * chip * share : 2 * (chip + 1) * share, :].astype(BF16)


def middle(terms, weight, cotangent):
    share = WIDTH // N_SRC
    vmem = pl.BlockSpec(memory_space=pltpu.VMEM)
    return pl.pallas_call(
        middle_kernel,
        out_shape=(
            jax.ShapeDtypeStruct((ROWS, WIDTH), BF16),
            jax.ShapeDtypeStruct((CHIPS, ROWS + 2 * share, WIDTH), BF16),
        ),
        in_specs=[vmem] * 3,
        out_specs=(vmem, vmem),
        compiler_params=pltpu.CompilerParams(vmem_limit_bytes=VMEM_LIMIT),
        name="middle",
    )(terms, weight, cotangent)


def backward_kernel(
    meta, coords, blocks, mine, theirs, kept0, kept1, kept2, kept3, sent0, sent13, sent2, wsum, rows, total
):
    slot_count, z, y, core = meta[0], meta[1], meta[2], meta[3]
    slots = blocks.shape[0]

    def one_slot(ks):
        terms = [
            jnp.dot(blocks[k], block_of(rows, coords[slots + k]), preferred_element_type=F32)
            for k in ks
        ]
        for k, term in zip(ks, terms):
            add_block(total, coords[k], term)

    share = wsum.shape[0]
    summed = jnp.zeros(wsum.shape, F32)
    for ref, owner in ((mine, core), (theirs, 1 - core)):
        for chip in range(CHIPS):
            place = pl.multiple_of((2 * chip + owner) * ROWS, ROWS)
            rows[pl.ds(place, ROWS), :] = ref[chip, :ROWS, :]
            tail = pl.ds(pl.multiple_of(ROWS + core * share, share), share)
            summed = summed + ref[chip, tail, :].astype(F32)
    wsum[...] = summed
    sent2[4 * ROWS :, :] = summed.astype(BF16)
    total[...] = jnp.zeros_like(total)
    each_slot(slot_count, one_slot)
    mirror = 1 - y
    lists = (
        (sent2, 0, 6, mirror), (sent13, 0, 1, mirror), (sent13, 4, 15, mirror), (sent0, 0, 0, mirror),
        (kept0, 0, 0, y), (kept1, 0, 1, y), (kept2, 0, 6, y), (kept3, 0, 15, y),
    )
    for ref, first, offset, side in lists:
        for member in range(4):
            place = lax.rem(z + offset + 4 * member, NZ) * PAIR + side * ROWS
            chunk = total[pl.ds(pl.multiple_of(place, ROWS), ROWS), :]
            ref[(first + member) * ROWS : (first + member + 1) * ROWS, :] = chunk.astype(BF16)


def backward_sums(meta, coords, values, mine, theirs):
    share = (mine.shape[1] - ROWS) // 2
    dest_rows = N_SRC * ROWS
    source_rows = NZ * PAIR
    smem = pl.BlockSpec(memory_space=pltpu.SMEM)
    vmem = pl.BlockSpec(memory_space=pltpu.VMEM)

    def rows_of(count):
        return jax.ShapeDtypeStruct((count, WIDTH), BF16)

    list_rows = 4 * ROWS
    out = pl.pallas_call(
        backward_kernel,
        out_shape=(rows_of(list_rows),) * 5
        + (rows_of(2 * list_rows), rows_of(list_rows + share), jax.ShapeDtypeStruct((share, WIDTH), F32)),
        in_specs=[smem, smem, vmem, vmem, vmem],
        out_specs=(vmem,) * 8,
        scratch_shapes=[pltpu.VMEM((dest_rows, WIDTH), BF16), pltpu.VMEM((source_rows, WIDTH), F32)],
        compiler_params=pltpu.CompilerParams(vmem_limit_bytes=VMEM_LIMIT),
        name="backward_sums",
    )(meta, coords, values, mine, theirs)
    return (out[:4],) + tuple(out[4:])


def shift(array, step):
    return lax.ppermute(array, "dst", from_z(step))


def gather_sources(features):
    own = lax.all_gather(features, "dst", axis=0, axis_index_groups=STRIDE_GROUPS)
    own = lax.all_gather(own, "dst", axis=1, tiled=True, axis_index_groups=Y_GROUPS)
    low, high = own[:2], own[2:]
    right_low, left_high = shift(low, 1), shift(high, -1)
    right_high, left_low = shift(high, 1), shift(low, -1)
    far_low, far_high = shift(right_low, 1), shift(left_high, -1)
    return own, right_low, right_high, far_low, far_high, left_low, left_high


def total_of(*terms):
    return sum(term.astype(F32) for term in terms).astype(BF16)


def total_f32(*terms):
    return sum(term.astype(F32) for term in terms)


def total_f32(*terms):
    return sum(term.astype(F32) for term in terms)


def pair_swap(array, axis, groups, side):
    both = lax.all_gather(array, axis, axis=0, axis_index_groups=groups)
    return lax.dynamic_index_in_dim(both, 1 - side, 0, keepdims=False)


def scatter_sources(kept, sent0, sent13, sent2, w, y):
    half, full = 2 * ROWS, 4 * ROWS
    swap2 = pair_swap(sent2, "dst", Y_GROUPS, y)
    swap13 = lax.ppermute(sent13, "dst", Y_SWAP)
    w = total_f32(w, swap2[full:])
    low = total_of(kept[2][:half], swap2[:half])
    high = jnp.concatenate([total_of(kept[2][half:], swap2[half:full]), w.astype(BF16)], 0)
    sent0, low, high = lax.optimization_barrier((sent0, low, high))
    low, high = shift(low, -1), shift(high, 1)
    swap0 = pair_swap(sent0, "dst", Y_GROUPS, y)
    w = total_of(w, high[half:])
    none = jnp.zeros_like(low[:ROWS])
    up = total_of(kept[1], swap13[:full], jnp.concatenate([none, low, none], 0))
    down = total_of(kept[3], swap13[full:], jnp.concatenate([high[:half], none, none], 0))
    up = shift(jnp.concatenate([up, w], 0), -1)
    down = shift(jnp.concatenate([down, w], 0), 1)
    w = total_of(up[full:], down[full:])
    near = total_of(kept[0], swap0, up[:full], down[:full]).reshape(4, ROWS, WIDTH)

    part = ROWS // 2
    from_left = shift(jnp.concatenate([near[2, :part], w], 0), -4)
    from_right = shift(jnp.concatenate([near[2, part:], w], 0), 4)
    w_left, w_right = from_left[part:], from_right[part:]
    none = jnp.zeros((part, WIDTH), BF16)
    left = shift(total_of(near[1], jnp.concatenate([from_left[:part], none], 0)), -4)
    right = total_of(near[3], jnp.concatenate([none, from_right[:part]], 0))
    right = shift(jnp.concatenate([right, w_right], 0), 4)
    w = total_of(w, w_left, w_right, right[ROWS:])
    return total_of(near[0], left, right[:ROWS]), w


def gather_weight(part):
    copies = jnp.broadcast_to(part, (N_SRC,) + part.shape)
    return lax.all_to_all(copies, "src", 0, 0, tiled=True).reshape(WIDTH, WIDTH).astype(F32)


def staged(meta, values):
    live = jnp.arange(values.shape[0], dtype=jnp.int32) < meta[0]
    return jnp.where(live[:, None, None], values, jnp.zeros((), BF16))


def shards(features, weight, values, coords, counts, cotangent):
    tile_values = values[0, 0]
    pairs = coords[0, 0].T.reshape(-1)
    place = lax.axis_index("dst")
    z, y, core = place // NY, lax.rem(place, NY), lax.rem(lax.axis_index("src"), 2)
    meta = jnp.stack([counts[0, 0], z, y, core]).astype(jnp.int32)
    dest_rows = cotangent.shape[1] * N_SRC

    parts = gather_sources(features)
    tile_values, _ = lax.optimization_barrier((tile_values, parts[0]))
    blocks = staged(meta, tile_values)
    own, other = forward_sums(meta, pairs, blocks, parts, dest_rows)
    swapped = lax.ppermute(other, "src", CORE_SWAP)
    chip_sums = (own.astype(F32) + swapped.astype(F32)).astype(BF16)
    terms = lax.all_to_all(
        chip_sums.reshape(CHIPS, ROWS, WIDTH), "src", 0, 0, tiled=True, axis_index_groups=CORE_GROUPS
    )
    activations, message = middle(terms, weight, cotangent[0])
    mine = lax.all_to_all(message, "src", 0, 0, tiled=True, axis_index_groups=CORE_GROUPS)
    theirs = lax.ppermute(mine, "src", CORE_SWAP)
    tile_values, mine = lax.optimization_barrier((values[0, 0], mine))
    sums = backward_sums(meta, pairs, staged(meta, tile_values), mine, theirs)
    input_grad, weight_part = scatter_sources(*sums, y)
    weight_grad = gather_weight(weight_part)
    return (activations[None], input_grad, weight_grad)


def solution(mesh):
    in_specs = (
        P(("src", "dst"), None),
        P(),
        P("src", "dst", None, None, None),
        P("src", "dst", None, None),
        P("src", "dst"),
        P("dst", "src", None),
    )
    out_specs = (P("dst", "src", None), P(("src", "dst"), None), P())
    return jax.shard_map(shards, mesh=mesh, in_specs=in_specs, out_specs=out_specs, check_vma=False)
```

```python
import functools

import jax
import jax.numpy as jnp
from jax import lax
from jax.experimental import pallas as pl
from jax.experimental.pallas import tpu as pltpu
from jax.sharding import PartitionSpec as P

BF16 = jnp.bfloat16
F32 = jnp.float32
NZ, NY = 16, 2
N_SRC = 16
SIDE = 128
WIDTH = 256
ROWS = 192
PAIR = NY * ROWS
VMEM_LIMIT = 24 * 1024 * 1024

STRIDE_GROUPS = [[2 * z + y for z in range(q, NZ, 4)] for q in range(4) for y in range(NY)]
Y_GROUPS = [[2 * z, 2 * z + 1] for z in range(NZ)]
Y_SWAP = [(d, d ^ 1) for d in range(NZ * NY)]
CHIPS = N_SRC // 2
CORE_GROUPS = [[2 * chip + core for chip in range(CHIPS)] for core in range(2)]
CORE_SWAP = [(s, s ^ 1) for s in range(N_SRC)]


def from_z(step):
    return [(((z + step) % NZ) * NY + y, z * NY + y) for z in range(NZ) for y in range(NY)]


def each_slot(slot_count, one_slot):
    done = 0
    for step in (36, 12, 4, 1):

        def several(i, carry, step=step, done=done):
            one_slot([done + i * step + u for u in range(step)])
            return carry

        turns = (slot_count - done) // step
        lax.fori_loop(0, turns, several, 0)
        done = done + turns * step


def block_of(ref, index):
    return ref[pl.ds(pl.multiple_of(index * SIDE, SIDE), SIDE), :]


def add_block(ref, index, term):
    span = pl.ds(pl.multiple_of(index * SIDE, SIDE), SIDE)
    ref[span, :] = ref[span, :] + term


def forward_kernel(meta, coords, blocks, g0, g1a, g1b, g2a, g2b, g3a, g3b, own, other, rows, total):
    slot_count, z, core = meta[0], meta[1], meta[3]
    slots = blocks.shape[0]

    def one_slot(ks):
        terms = [
            lax.dot_general(
                blocks[k], block_of(rows, coords[0, k]), (((0,), (0,)), ((), ())), preferred_element_type=F32
            )
            for k in ks
        ]
        for k, term in zip(ks, terms):
            add_block(total, coords[1, k], term)

    pieces = ((0, g0, 0), (1, g1a, 0), (1, g1b, 2), (2, g2a, 0), (2, g2b, 2), (3, g3a, 0), (3, g3b, 2))
    for offset, ref, first in pieces:
        residue = lax.rem(z + offset, 4)
        for i in range(ref.shape[0]):
            place = pl.multiple_of((residue + 4 * (first + i)) * PAIR, PAIR)
            rows[pl.ds(place, PAIR), :] = ref[i]
    total[...] = jnp.zeros_like(total)
    each_slot(slot_count, one_slot)
    for chip in range(CHIPS):
        for ref, target in ((own, core), (other, 1 - core)):
            place = pl.multiple_of((2 * chip + target) * ROWS, ROWS)
            ref[chip * ROWS : (chip + 1) * ROWS, :] = total[pl.ds(place, ROWS), :].astype(BF16)


def forward_sums(meta, coords, values, parts, dest_rows):
    source_rows = NZ * PAIR
    smem = pl.BlockSpec(memory_space=pltpu.SMEM)
    vmem = pl.BlockSpec(memory_space=pltpu.VMEM)
    half = jax.ShapeDtypeStruct((dest_rows // 2, WIDTH), BF16)
    return pl.pallas_call(
        forward_kernel,
        out_shape=(half, half),
        in_specs=[smem, smem] + [vmem] * 8,
        out_specs=(vmem, vmem),
        scratch_shapes=[pltpu.VMEM((source_rows, WIDTH), BF16), pltpu.VMEM((dest_rows, WIDTH), F32)],
        compiler_params=pltpu.CompilerParams(vmem_limit_bytes=VMEM_LIMIT),
        name="forward_sums",
    )(meta, coords, values, *parts)


def middle_kernel(terms, weight, cotangent, act_ref, message):
    agg = jnp.sum(terms[...].astype(F32), axis=0).astype(BF16)
    w = weight[...]
    preact = jnp.dot(agg, w, preferred_element_type=F32)
    sigma = jax.nn.sigmoid(preact)
    act_ref[...] = (preact * sigma).astype(BF16)
    slope = sigma * (1.0 + preact * (1.0 - sigma))
    delta = (cotangent[...].astype(F32) * slope).astype(BF16)
    grad_agg = lax.dot_general(
        delta, w, (((1,), (1,)), ((), ())), preferred_element_type=F32
    ).astype(BF16)
    local = lax.dot_general(agg, delta, (((0,), (0,)), ((), ())), preferred_element_type=F32)
    share = WIDTH // N_SRC
    for chip in range(CHIPS):
        message[chip, :ROWS, :] = grad_agg
        message[chip, ROWS:, :] = local[2 * chip * share : 2 * (chip + 1) * share, :].astype(BF16)


def middle(terms, weight, cotangent):
    share = WIDTH // N_SRC
    vmem = pl.BlockSpec(memory_space=pltpu.VMEM)
    return pl.pallas_call(
        middle_kernel,
        out_shape=(
            jax.ShapeDtypeStruct((ROWS, WIDTH), BF16),
            jax.ShapeDtypeStruct((CHIPS, ROWS + 2 * share, WIDTH), BF16),
        ),
        in_specs=[vmem] * 3,
        out_specs=(vmem, vmem),
        compiler_params=pltpu.CompilerParams(vmem_limit_bytes=VMEM_LIMIT),
        name="middle",
    )(terms, weight, cotangent)


def backward_kernel(
    meta, coords, blocks, mine, theirs, kept0, kept1, kept2, kept3, sent0, sent13, sent2, wsum, rows, total
):
    slot_count, z, y, core = meta[0], meta[1], meta[2], meta[3]
    slots = blocks.shape[0]

    def one_slot(ks):
        terms = [
            jnp.dot(blocks[k], block_of(rows, coords[1, k]), preferred_element_type=F32)
            for k in ks
        ]
        for k, term in zip(ks, terms):
            add_block(total, coords[0, k], term)

    share = wsum.shape[0]
    summed = jnp.zeros(wsum.shape, F32)
    for ref, owner in ((mine, core), (theirs, 1 - core)):
        for chip in range(CHIPS):
            place = pl.multiple_of((2 * chip + owner) * ROWS, ROWS)
            rows[pl.ds(place, ROWS), :] = ref[chip, :ROWS, :]
            tail = pl.ds(pl.multiple_of(ROWS + core * share, share), share)
            summed = summed + ref[chip, tail, :].astype(F32)
    wsum[...] = summed
    sent2[4 * ROWS :, :] = summed.astype(BF16)
    total[...] = jnp.zeros_like(total)
    each_slot(slot_count, one_slot)
    mirror = 1 - y
    lists = (
        (sent2, 0, 6, mirror), (sent13, 0, 1, mirror), (sent13, 4, 15, mirror), (sent0, 0, 0, mirror),
        (kept0, 0, 0, y), (kept1, 0, 1, y), (kept2, 0, 6, y), (kept3, 0, 15, y),
    )
    for ref, first, offset, side in lists:
        for member in range(4):
            place = lax.rem(z + offset + 4 * member, NZ) * PAIR + side * ROWS
            chunk = total[pl.ds(pl.multiple_of(place, ROWS), ROWS), :]
            ref[(first + member) * ROWS : (first + member + 1) * ROWS, :] = chunk.astype(BF16)


def backward_sums(meta, coords, values, mine, theirs):
    share = (mine.shape[1] - ROWS) // 2
    dest_rows = N_SRC * ROWS
    source_rows = NZ * PAIR
    smem = pl.BlockSpec(memory_space=pltpu.SMEM)
    vmem = pl.BlockSpec(memory_space=pltpu.VMEM)

    def rows_of(count):
        return jax.ShapeDtypeStruct((count, WIDTH), BF16)

    list_rows = 4 * ROWS
    out = pl.pallas_call(
        backward_kernel,
        out_shape=(rows_of(list_rows),) * 5
        + (rows_of(2 * list_rows), rows_of(list_rows + share), jax.ShapeDtypeStruct((share, WIDTH), F32)),
        in_specs=[smem, smem, vmem, vmem, vmem],
        out_specs=(vmem,) * 8,
        scratch_shapes=[pltpu.VMEM((dest_rows, WIDTH), BF16), pltpu.VMEM((source_rows, WIDTH), F32)],
        compiler_params=pltpu.CompilerParams(vmem_limit_bytes=VMEM_LIMIT),
        name="backward_sums",
    )(meta, coords, values, mine, theirs)
    return (out[:4],) + tuple(out[4:])


def shift(array, step):
    return lax.ppermute(array, "dst", from_z(step))


def gather_sources(features):
    own = lax.all_gather(features, "dst", axis=0, axis_index_groups=STRIDE_GROUPS)
    own = lax.all_gather(own, "dst", axis=1, tiled=True, axis_index_groups=Y_GROUPS)
    low, high = own[:2], own[2:]
    right_low, left_high = shift(low, 1), shift(high, -1)
    right_high, left_low = shift(high, 1), shift(low, -1)
    far_low, far_high = shift(right_low, 1), shift(left_high, -1)
    return own, right_low, right_high, far_low, far_high, left_low, left_high


def total_of(*terms):
    return sum(term.astype(F32) for term in terms).astype(BF16)


def total_f32(*terms):
    return sum(term.astype(F32) for term in terms)


def total_f32(*terms):
    return sum(term.astype(F32) for term in terms)


def pair_swap(array, axis, groups, side):
    both = lax.all_gather(array, axis, axis=0, axis_index_groups=groups)
    return lax.dynamic_index_in_dim(both, 1 - side, 0, keepdims=False)


def scatter_sources(kept, sent0, sent13, sent2, w, y):
    half, full = 2 * ROWS, 4 * ROWS
    swap2 = pair_swap(sent2, "dst", Y_GROUPS, y)
    swap13 = lax.ppermute(sent13, "dst", Y_SWAP)
    w = total_f32(w, swap2[full:])
    low = total_of(kept[2][:half], swap2[:half])
    high = jnp.concatenate([total_of(kept[2][half:], swap2[half:full]), w.astype(BF16)], 0)
    sent0, low, high = lax.optimization_barrier((sent0, low, high))
    low, high = shift(low, -1), shift(high, 1)
    swap0 = pair_swap(sent0, "dst", Y_GROUPS, y)
    w = total_of(w, high[half:])
    none = jnp.zeros_like(low[:ROWS])
    up = total_of(kept[1], swap13[:full], jnp.concatenate([none, low, none], 0))
    down = total_of(kept[3], swap13[full:], jnp.concatenate([high[:half], none, none], 0))
    up = shift(jnp.concatenate([up, w], 0), -1)
    down = shift(jnp.concatenate([down, w], 0), 1)
    w = total_of(up[full:], down[full:])
    near = total_of(kept[0], swap0, up[:full], down[:full]).reshape(4, ROWS, WIDTH)

    part = ROWS // 2
    from_left = shift(jnp.concatenate([near[2, :part], w], 0), -4)
    from_right = shift(jnp.concatenate([near[2, part:], w], 0), 4)
    w_left, w_right, w_far = from_left[part:], from_right[part:], shift(w, 8)
    none = jnp.zeros((part, WIDTH), BF16)
    left = shift(total_of(near[1], jnp.concatenate([from_left[:part], none], 0)), -4)
    right = total_of(near[3], jnp.concatenate([none, from_right[:part]], 0))
    right = shift(right, 4)
    return total_of(near[0], left, right), total_of(w, w_left, w_right, w_far)


def gather_weight(part):
    copies = jnp.broadcast_to(part, (N_SRC,) + part.shape)
    return lax.all_to_all(copies, "src", 0, 0, tiled=True).reshape(WIDTH, WIDTH).astype(F32)


def staged(meta, values):
    live = jnp.arange(values.shape[0], dtype=jnp.int32) < meta[0]
    return jnp.where(live[:, None, None], values, jnp.zeros((), BF16))


def shards(features, weight, values, coords, counts, cotangent):
    tile_values = values[0, 0]
    pairs = coords[0, 0].T
    place = lax.axis_index("dst")
    z, y, core = place // NY, lax.rem(place, NY), lax.rem(lax.axis_index("src"), 2)
    meta = jnp.stack([counts[0, 0], z, y, core]).astype(jnp.int32)
    dest_rows = cotangent.shape[1] * N_SRC

    parts = gather_sources(features)
    tile_values, _ = lax.optimization_barrier((tile_values, parts[0]))
    blocks = staged(meta, tile_values)
    own, other = forward_sums(meta, pairs, blocks, parts, dest_rows)
    swapped = lax.ppermute(other, "src", CORE_SWAP)
    chip_sums = (own.astype(F32) + swapped.astype(F32)).astype(BF16)
    terms = lax.all_to_all(
        chip_sums.reshape(CHIPS, ROWS, WIDTH), "src", 0, 0, tiled=True, axis_index_groups=CORE_GROUPS
    )
    activations, message = middle(terms, weight, cotangent[0])
    mine = lax.all_to_all(message, "src", 0, 0, tiled=True, axis_index_groups=CORE_GROUPS)
    theirs = lax.ppermute(mine, "src", CORE_SWAP)
    tile_values, mine = lax.optimization_barrier((values[0, 0], mine))
    sums = backward_sums(meta, pairs, staged(meta, tile_values), mine, theirs)
    input_grad, weight_part = scatter_sources(*sums, y)
    weight_grad = gather_weight(weight_part)
    return (activations[None], input_grad, weight_grad)


def solution(mesh):
    in_specs = (
        P(("src", "dst"), None),
        P(),
        P("src", "dst", None, None, None),
        P("src", "dst", None, None),
        P("src", "dst"),
        P("dst", "src", None),
    )
    out_specs = (P("dst", "src", None), P(("src", "dst"), None), P())
    return jax.shard_map(shards, mesh=mesh, in_specs=in_specs, out_specs=out_specs, check_vma=False)
```

```python
import functools

import jax
import jax.numpy as jnp
from jax import lax
from jax.experimental import pallas as pl
from jax.experimental.pallas import tpu as pltpu
from jax.sharding import PartitionSpec as P

BF16 = jnp.bfloat16
F32 = jnp.float32
NZ, NY = 16, 2
N_SRC = 16
SIDE = 128
WIDTH = 256
ROWS = 192
PAIR = NY * ROWS
VMEM_LIMIT = 24 * 1024 * 1024

STRIDE_GROUPS = [[2 * z + y for z in range(q, NZ, 4)] for q in range(4) for y in range(NY)]
Y_GROUPS = [[2 * z, 2 * z + 1] for z in range(NZ)]
Y_SWAP = [(d, d ^ 1) for d in range(NZ * NY)]
CHIPS = N_SRC // 2
CORE_GROUPS = [[2 * chip + core for chip in range(CHIPS)] for core in range(2)]
CORE_SWAP = [(s, s ^ 1) for s in range(N_SRC)]


def from_z(step):
    return [(((z + step) % NZ) * NY + y, z * NY + y) for z in range(NZ) for y in range(NY)]


def each_slot(slot_count, one_slot):
    done = 0
    for step in (48, 16, 4, 1):

        def several(i, carry, step=step, done=done):
            one_slot([done + i * step + u for u in range(step)])
            return carry

        turns = (slot_count - done) // step
        lax.fori_loop(0, turns, several, 0)
        done = done + turns * step


def block_of(ref, index):
    return ref[pl.ds(pl.multiple_of(index * SIDE, SIDE), SIDE), :]


def add_block(ref, index, term):
    span = pl.ds(pl.multiple_of(index * SIDE, SIDE), SIDE)
    ref[span, :] = ref[span, :] + term


def forward_kernel(meta, coords, blocks, g0, g1a, g1b, g2a, g2b, g3a, g3b, own, other, rows, total):
    slot_count, z, core = meta[0], meta[1], meta[3]
    slots = blocks.shape[0]

    def one_slot(ks):
        terms = [
            lax.dot_general(
                blocks[k], block_of(rows, coords[0, k]), (((0,), (0,)), ((), ())), preferred_element_type=F32
            )
            for k in ks
        ]
        for k, term in zip(ks, terms):
            add_block(total, coords[1, k], term)

    pieces = ((0, g0, 0), (1, g1a, 0), (1, g1b, 2), (2, g2a, 0), (2, g2b, 2), (3, g3a, 0), (3, g3b, 2))
    for offset, ref, first in pieces:
        residue = lax.rem(z + offset, 4)
        for i in range(ref.shape[0]):
            place = pl.multiple_of((residue + 4 * (first + i)) * PAIR, PAIR)
            rows[pl.ds(place, PAIR), :] = ref[i]
    total[...] = jnp.zeros_like(total)
    each_slot(slot_count, one_slot)
    for chip in range(CHIPS):
        for ref, target in ((own, core), (other, 1 - core)):
            place = pl.multiple_of((2 * chip + target) * ROWS, ROWS)
            ref[chip * ROWS : (chip + 1) * ROWS, :] = total[pl.ds(place, ROWS), :].astype(BF16)


def forward_sums(meta, coords, values, parts, dest_rows):
    source_rows = NZ * PAIR
    smem = pl.BlockSpec(memory_space=pltpu.SMEM)
    vmem = pl.BlockSpec(memory_space=pltpu.VMEM)
    half = jax.ShapeDtypeStruct((dest_rows // 2, WIDTH), BF16)
    return pl.pallas_call(
        forward_kernel,
        out_shape=(half, half),
        in_specs=[smem, smem] + [vmem] * 8,
        out_specs=(vmem, vmem),
        scratch_shapes=[pltpu.VMEM((source_rows, WIDTH), BF16), pltpu.VMEM((dest_rows, WIDTH), F32)],
        compiler_params=pltpu.CompilerParams(vmem_limit_bytes=VMEM_LIMIT),
        name="forward_sums",
    )(meta, coords, values, *parts)


def middle_kernel(terms, weight, cotangent, act_ref, message):
    agg = jnp.sum(terms[...].astype(F32), axis=0).astype(BF16)
    w = weight[...]
    preact = jnp.dot(agg, w, preferred_element_type=F32)
    sigma = jax.nn.sigmoid(preact)
    act_ref[...] = (preact * sigma).astype(BF16)
    slope = sigma * (1.0 + preact * (1.0 - sigma))
    delta = (cotangent[...].astype(F32) * slope).astype(BF16)
    grad_agg = lax.dot_general(
        delta, w, (((1,), (1,)), ((), ())), preferred_element_type=F32
    ).astype(BF16)
    local = lax.dot_general(agg, delta, (((0,), (0,)), ((), ())), preferred_element_type=F32)
    share = WIDTH // N_SRC
    for chip in range(CHIPS):
        message[chip, :ROWS, :] = grad_agg
        message[chip, ROWS:, :] = local[2 * chip * share : 2 * (chip + 1) * share, :].astype(BF16)


def middle(terms, weight, cotangent):
    share = WIDTH // N_SRC
    vmem = pl.BlockSpec(memory_space=pltpu.VMEM)
    return pl.pallas_call(
        middle_kernel,
        out_shape=(
            jax.ShapeDtypeStruct((ROWS, WIDTH), BF16),
            jax.ShapeDtypeStruct((CHIPS, ROWS + 2 * share, WIDTH), BF16),
        ),
        in_specs=[vmem] * 3,
        out_specs=(vmem, vmem),
        compiler_params=pltpu.CompilerParams(vmem_limit_bytes=VMEM_LIMIT),
        name="middle",
    )(terms, weight, cotangent)


def backward_kernel(
    meta, coords, blocks, mine, theirs, kept0, kept1, kept2, kept3, sent0, sent13, sent2, wsum, rows, total
):
    slot_count, z, y, core = meta[0], meta[1], meta[2], meta[3]
    slots = blocks.shape[0]

    def one_slot(ks):
        terms = [
            jnp.dot(blocks[k], block_of(rows, coords[1, k]), preferred_element_type=F32)
            for k in ks
        ]
        for k, term in zip(ks, terms):
            add_block(total, coords[0, k], term)

    share = wsum.shape[0]
    summed = jnp.zeros(wsum.shape, F32)
    for ref, owner in ((mine, core), (theirs, 1 - core)):
        for chip in range(CHIPS):
            place = pl.multiple_of((2 * chip + owner) * ROWS, ROWS)
            rows[pl.ds(place, ROWS), :] = ref[chip, :ROWS, :]
            tail = pl.ds(pl.multiple_of(ROWS + core * share, share), share)
            summed = summed + ref[chip, tail, :].astype(F32)
    wsum[...] = summed
    sent2[4 * ROWS :, :] = summed.astype(BF16)
    total[...] = jnp.zeros_like(total)
    each_slot(slot_count, one_slot)
    mirror = 1 - y
    lists = (
        (sent2, 0, 6, mirror), (sent13, 0, 1, mirror), (sent13, 4, 15, mirror), (sent0, 0, 0, mirror),
        (kept0, 0, 0, y), (kept1, 0, 1, y), (kept2, 0, 6, y), (kept3, 0, 15, y),
    )
    for ref, first, offset, side in lists:
        for member in range(4):
            place = lax.rem(z + offset + 4 * member, NZ) * PAIR + side * ROWS
            chunk = total[pl.ds(pl.multiple_of(place, ROWS), ROWS), :]
            ref[(first + member) * ROWS : (first + member + 1) * ROWS, :] = chunk.astype(BF16)


def backward_sums(meta, coords, values, mine, theirs):
    share = (mine.shape[1] - ROWS) // 2
    dest_rows = N_SRC * ROWS
    source_rows = NZ * PAIR
    smem = pl.BlockSpec(memory_space=pltpu.SMEM)
    vmem = pl.BlockSpec(memory_space=pltpu.VMEM)

    def rows_of(count):
        return jax.ShapeDtypeStruct((count, WIDTH), BF16)

    list_rows = 4 * ROWS
    out = pl.pallas_call(
        backward_kernel,
        out_shape=(rows_of(list_rows),) * 5
        + (rows_of(2 * list_rows), rows_of(list_rows + share), jax.ShapeDtypeStruct((share, WIDTH), F32)),
        in_specs=[smem, smem, vmem, vmem, vmem],
        out_specs=(vmem,) * 8,
        scratch_shapes=[pltpu.VMEM((dest_rows, WIDTH), BF16), pltpu.VMEM((source_rows, WIDTH), F32)],
        compiler_params=pltpu.CompilerParams(vmem_limit_bytes=VMEM_LIMIT),
        name="backward_sums",
    )(meta, coords, values, mine, theirs)
    return (out[:4],) + tuple(out[4:])


def shift(array, step):
    return lax.ppermute(array, "dst", from_z(step))


def gather_sources(features):
    own = lax.all_gather(features, "dst", axis=0, axis_index_groups=STRIDE_GROUPS)
    own = lax.all_gather(own, "dst", axis=1, tiled=True, axis_index_groups=Y_GROUPS)
    low, high = own[:2], own[2:]
    right_low, left_high = shift(low, 1), shift(high, -1)
    right_high, left_low = shift(high, 1), shift(low, -1)
    far_low, far_high = shift(right_low, 1), shift(left_high, -1)
    return own, right_low, right_high, far_low, far_high, left_low, left_high


def total_of(*terms):
    return sum(term.astype(F32) for term in terms).astype(BF16)


def total_f32(*terms):
    return sum(term.astype(F32) for term in terms)


def total_f32(*terms):
    return sum(term.astype(F32) for term in terms)


def pair_swap(array, axis, groups, side):
    both = lax.all_gather(array, axis, axis=0, axis_index_groups=groups)
    return lax.dynamic_index_in_dim(both, 1 - side, 0, keepdims=False)


def scatter_sources(kept, sent0, sent13, sent2, w, y):
    half, full = 2 * ROWS, 4 * ROWS
    swap2 = pair_swap(sent2, "dst", Y_GROUPS, y)
    swap13 = lax.ppermute(sent13, "dst", Y_SWAP)
    w = total_f32(w, swap2[full:])
    low = total_of(kept[2][:half], swap2[:half])
    high = jnp.concatenate([total_of(kept[2][half:], swap2[half:full]), w.astype(BF16)], 0)
    sent0, low, high = lax.optimization_barrier((sent0, low, high))
    low, high = shift(low, -1), shift(high, 1)
    swap0 = pair_swap(sent0, "dst", Y_GROUPS, y)
    w = total_of(w, high[half:])
    none = jnp.zeros_like(low[:ROWS])
    up = total_of(kept[1], swap13[:full], jnp.concatenate([none, low, none], 0))
    down = total_of(kept[3], swap13[full:], jnp.concatenate([high[:half], none, none], 0))
    up = shift(jnp.concatenate([up, w], 0), -1)
    down = shift(jnp.concatenate([down, w], 0), 1)
    w = total_of(up[full:], down[full:])
    near = total_of(kept[0], swap0, up[:full], down[:full]).reshape(4, ROWS, WIDTH)

    part = ROWS // 2
    from_left = shift(jnp.concatenate([near[2, :part], w], 0), -4)
    from_right = shift(jnp.concatenate([near[2, part:], w], 0), 4)
    w_left, w_right, w_far = from_left[part:], from_right[part:], shift(w, 8)
    none = jnp.zeros((part, WIDTH), BF16)
    left = shift(total_of(near[1], jnp.concatenate([from_left[:part], none], 0)), -4)
    right = total_of(near[3], jnp.concatenate([none, from_right[:part]], 0))
    right = shift(right, 4)
    return total_of(near[0], left, right), total_of(w, w_left, w_right, w_far)


def gather_weight(part):
    copies = jnp.broadcast_to(part, (N_SRC,) + part.shape)
    return lax.all_to_all(copies, "src", 0, 0, tiled=True).reshape(WIDTH, WIDTH).astype(F32)


def staged(meta, values):
    live = jnp.arange(values.shape[0], dtype=jnp.int32) < meta[0]
    return jnp.where(live[:, None, None], values, jnp.zeros((), BF16))


def shards(features, weight, values, coords, counts, cotangent):
    tile_values = values[0, 0]
    pairs = coords[0, 0].T
    place = lax.axis_index("dst")
    z, y, core = place // NY, lax.rem(place, NY), lax.rem(lax.axis_index("src"), 2)
    meta = jnp.stack([counts[0, 0], z, y, core]).astype(jnp.int32)
    dest_rows = cotangent.shape[1] * N_SRC

    parts = gather_sources(features)
    tile_values, _ = lax.optimization_barrier((tile_values, parts[0]))
    blocks = staged(meta, tile_values)
    own, other = forward_sums(meta, pairs, blocks, parts, dest_rows)
    swapped = lax.ppermute(other, "src", CORE_SWAP)
    chip_sums = (own.astype(F32) + swapped.astype(F32)).astype(BF16)
    terms = lax.all_to_all(
        chip_sums.reshape(CHIPS, ROWS, WIDTH), "src", 0, 0, tiled=True, axis_index_groups=CORE_GROUPS
    )
    activations, message = middle(terms, weight, cotangent[0])
    mine = lax.all_to_all(message, "src", 0, 0, tiled=True, axis_index_groups=CORE_GROUPS)
    theirs = lax.ppermute(mine, "src", CORE_SWAP)
    tile_values, mine = lax.optimization_barrier((values[0, 0], mine))
    sums = backward_sums(meta, pairs, staged(meta, tile_values), mine, theirs)
    input_grad, weight_part = scatter_sources(*sums, y)
    weight_grad = gather_weight(weight_part)
    return (activations[None], input_grad, weight_grad)


def solution(mesh):
    in_specs = (
        P(("src", "dst"), None),
        P(),
        P("src", "dst", None, None, None),
        P("src", "dst", None, None),
        P("src", "dst"),
        P("dst", "src", None),
    )
    out_specs = (P("dst", "src", None), P(("src", "dst"), None), P())
    return jax.shard_map(shards, mesh=mesh, in_specs=in_specs, out_specs=out_specs, check_vma=False)
```
